256 devices in a mesh: row: 8 (over x_lo, y), col: 32 (over z, x_hi, core).
Axes of the slice: x: 4 (x_hi: 2, x_lo: 2; x = x_hi * 2 + x_lo), y: 4, z: 8, core: 2. Of those that a mesh axis runs over, the one named last changes fastest.
Arguments:
- queries: bfloat16 [128, 256, 1024], P('row', 'col'), may hold values from -16 to 16
- keys: bfloat16 [128, 256, 1024], P('row', 'col'), may hold values from -16 to 16
- values: bfloat16 [128, 256, 1024], P('row', 'col'), may hold values from -6 to 6
- grad_out: bfloat16 [128, 256, 1024], P('row', 'col'), may hold values from -190 to 190
- out_weight: bfloat16 [1024, 1024], replicated, may hold values from -0.1875 to 0.1875
- rel_bias: float32 [16, 121], replicated, may hold values from -4 to 4
Outputs:
- grad_queries: bfloat16 [128, 256, 1024], P('row', 'col')
- grad_keys: bfloat16 [128, 256, 1024], P('row', 'col')
- grad_values: bfloat16 [128, 256, 1024], P('row', 'col')
- grad_out_weight: bfloat16 [1024, 1024], replicated
- grad_bias: float32 [16, 121], replicated
The draws below stay inside these ranges and needn't reach their ends.
All inputs are finite; a program needn't handle non-finite values.
Results may differ from the reference program's by a relative error of at most 0.0068.
Values may be sent and summed in bfloat16 or wider, within the bound.
A program may use at most 128 MiB of HBM per device.

```python
import math
import jax
import jax.numpy as jnp
import numpy as np
from jax import lax

D = 1024
HEADS = 16
RAD = 5
KS = 11
CH = 16
CW = 8
H = 128
W = 256


def draw_queries(key, part):
    key = jax.random.fold_in(key, 1)
    result = jax.random.truncated_normal(key, -6.0, 6.0, (H, W, D), jnp.float32)
    return result.astype(jnp.bfloat16)


def draw_keys(key, part):
    key = jax.random.fold_in(key, 2)
    result = jax.random.truncated_normal(key, -6.0, 6.0, (H, W, D), jnp.float32)
    return result.astype(jnp.bfloat16)


def draw_grad_out(key, part):
    key = jax.random.fold_in(key, 3)
    token_scale = 10.0 ** (jax.random.uniform(jax.random.fold_in(key, 11), (H, W, 1), jnp.float32) - 0.5)
    feature_scale = 10.0 ** (jax.random.uniform(jax.random.fold_in(key, 12), (1, 1, D), jnp.float32) - 0.5)
    row_place = jnp.arange(H, dtype=jnp.float32)[:, None, None] / H
    col_place = jnp.arange(W, dtype=jnp.float32)[None, :, None] / W
    position_ramp = 3.0 ** (row_place + col_place) / 3.0
    result = jax.random.truncated_normal(jax.random.fold_in(key, 13), -6.0, 6.0, (H, W, D), jnp.float32)
    return (result * token_scale * feature_scale * position_ramp).astype(jnp.bfloat16)


def level_of(key, shape, pieces, smallest, high):
    def one(axis_at, shards_of):
        heights = jax.random.uniform(jax.random.fold_in(jax.random.fold_in(key, 6), axis_at), (shards_of,), jnp.float32, smallest / len(pieces), high / len(pieces))
        return jnp.repeat(jnp.exp(heights), shape[axis_at] // shards_of).reshape((-1,) + (1,) * (len(shape) - axis_at - 1))

    factor_of = one(*pieces[0])
    for cut in pieces[1:]:
        factor_of = factor_of * one(*cut)
    return factor_of


def scatter_about(rng, extent, deviation, most, split=(), held_as=jnp.bfloat16):
    array = deviation * jax.random.normal(rng, extent, jnp.float32)
    if split:
        array = array * level_of(rng, extent, split, -0.22, 0.18)
    return jnp.clip(array, -most, most).astype(held_as)


def setup_inputs(seed: int = 0) -> dict:
    seeds = jax.random.split(jax.random.key(seed), 7)
    return {
        "queries": draw_queries(jax.random.fold_in(seeds[6], 71), 0),
        "keys": draw_keys(jax.random.fold_in(seeds[6], 71), 0),
        "values": scatter_about(seeds[2], (H, W, D), 1.0, 6.0, ((0, 8), (1, 32))),
        "grad_out": draw_grad_out(jax.random.fold_in(seeds[6], 71), 0),
        "out_weight": scatter_about(seeds[4], (D, D), D ** -0.5, 0.1875),
        "rel_bias": scatter_about(seeds[5], (HEADS, KS * KS), 1.0, 4.0, (), jnp.float32),
    }


def offset_table(query_rows, query_cols, radius):
    window_side = 2 * radius + 1
    key_rows = query_rows + 2 * radius
    key_cols = query_cols + 2 * radius
    query_row = np.repeat(np.arange(query_rows), query_cols)
    query_col = np.tile(np.arange(query_cols), query_rows)
    key_row = np.repeat(np.arange(key_rows), key_cols)
    key_col = np.tile(np.arange(key_cols), key_rows)
    row_step = key_row[None, :] - radius - query_row[:, None]
    col_step = key_col[None, :] - radius - query_col[:, None]
    inside = (np.abs(row_step) <= radius) & (np.abs(col_step) <= radius)
    offsets = np.where(inside, (row_step + radius) * window_side + col_step + radius, window_side * window_side)
    return (offsets.astype(np.int32), inside)

def key_block_mask(first_row, first_col, key_rows, key_cols, total_rows, total_cols):
    rows_global = first_row + jnp.arange(key_rows, dtype=jnp.int32)
    cols_global = first_col + jnp.arange(key_cols, dtype=jnp.int32)
    inside_rows = (rows_global >= 0) & (rows_global < total_rows)
    inside_cols = (cols_global >= 0) & (cols_global < total_cols)
    return (inside_rows[:, None] & inside_cols[None, :]).reshape(-1)

def fold_offsets(score_grad, offsets, window_side):
    flat_grads = score_grad.reshape(score_grad.shape[0], -1).T
    offset_ids = jnp.asarray(offsets.reshape(-1))
    summed = jax.ops.segment_sum(flat_grads, offset_ids, num_segments=window_side * window_side + 1)
    return summed[:window_side * window_side].T

def attend_block(queries, keys, values, grad_attn, bias_rows, allowed, score_scale):
    wide = jnp.float32
    scores = jnp.einsum('qhd,khd->hqk', queries.astype(wide), keys.astype(wide)) * score_scale + bias_rows
    scores = jnp.where(allowed[None], scores, -1e+30)
    highest = lax.optimization_barrier(jnp.max(scores, axis=-1, keepdims=True))
    weights = jnp.where(allowed[None], jnp.exp(scores - highest), 0.0)
    probabilities = weights / lax.optimization_barrier(jnp.sum(weights, axis=-1, keepdims=True))
    probs_low = probabilities.astype(jnp.bfloat16)
    attended = jnp.einsum('hqk,khd->qhd', probs_low.astype(wide), values.astype(wide)).astype(jnp.bfloat16)
    prob_grad = jnp.einsum('qhd,khd->hqk', grad_attn.astype(wide), values.astype(wide))
    center = lax.optimization_barrier(jnp.sum(probabilities * prob_grad, axis=-1, keepdims=True))
    score_grad = probabilities * (prob_grad - center)
    score_low = score_grad.astype(jnp.bfloat16)
    grad_query = (jnp.einsum('hqk,khd->qhd', score_low.astype(wide), keys.astype(wide)) * score_scale).astype(jnp.bfloat16)
    key_part = jnp.einsum('hqk,qhd->khd', score_low.astype(wide), queries.astype(wide)) * score_scale
    value_part = jnp.einsum('hqk,qhd->khd', probs_low.astype(wide), grad_attn.astype(wide))
    return (attended, grad_query, key_part, value_part, score_grad)

def reference(queries, keys, values, grad_out, out_weight, rel_bias):
    total_rows, total_cols, model_width = queries.shape
    head_count = rel_bias.shape[0]
    head_size = model_width // head_count
    score_scale = 1.0 / math.sqrt(head_size)
    half_rows = CH // 2
    block_cols = CW
    key_rows = half_rows + 2 * RAD
    key_cols = block_cols + 2 * RAD
    grad_attn = jnp.dot(grad_out.reshape(-1, model_width), out_weight.T, preferred_element_type=jnp.float32)
    grad_attn = grad_attn.astype(jnp.bfloat16).reshape(total_rows, total_cols, model_width)
    padding = ((RAD, RAD), (RAD, RAD), (0, 0))
    padded_keys = jnp.pad(keys, padding)
    padded_values = jnp.pad(values, padding)
    offsets, inside = offset_table(half_rows, block_cols, RAD)
    clipped = np.minimum(offsets, KS * KS - 1)
    bias_rows = rel_bias[:, clipped]
    inside_mask = jnp.asarray(inside)
    across = total_cols // block_cols
    tile_count = total_rows // half_rows * across

    def one_tile(state_carry, tile_index):
        key_grad, value_grad, score_total = state_carry
        tile_row = tile_index // across * half_rows
        tile_col = tile_index % across * block_cols
        start = (tile_row, tile_col, jnp.int32(0))
        query_block = lax.dynamic_slice(queries, start, (half_rows, block_cols, model_width)).reshape(-1, head_count, head_size)
        grad_block = lax.dynamic_slice(grad_attn, start, (half_rows, block_cols, model_width)).reshape(-1, head_count, head_size)
        key_block = lax.dynamic_slice(padded_keys, start, (key_rows, key_cols, model_width)).reshape(-1, head_count, head_size)
        value_block = lax.dynamic_slice(padded_values, start, (key_rows, key_cols, model_width)).reshape(-1, head_count, head_size)
        allowed = inside_mask & key_block_mask(tile_row - RAD, tile_col - RAD, key_rows, key_cols, total_rows, total_cols)[None, :]
        attended, grad_query, key_part, value_part, score_grad = attend_block(query_block, key_block, value_block, grad_block, bias_rows, allowed, score_scale)
        old_keys = lax.dynamic_slice(key_grad, start, (key_rows, key_cols, model_width))
        key_grad = lax.dynamic_update_slice(key_grad, old_keys + key_part.reshape(key_rows, key_cols, model_width), start)
        old_values = lax.dynamic_slice(value_grad, start, (key_rows, key_cols, model_width))
        value_grad = lax.dynamic_update_slice(value_grad, old_values + value_part.reshape(key_rows, key_cols, model_width), start)
        return ((key_grad, value_grad, score_total + score_grad), (attended, grad_query))
    zeros_padded = jnp.zeros((total_rows + 2 * RAD, total_cols + 2 * RAD, model_width), jnp.float32)
    zeros_scores = jnp.zeros((head_count, half_rows * block_cols, key_rows * key_cols), jnp.float32)
    final, tiles = lax.scan(one_tile, (zeros_padded, zeros_padded, zeros_scores), jnp.arange(tile_count, dtype=jnp.int32))
    key_grad, value_grad, score_total = final

    def untile(stacked):
        shaped = stacked.reshape(total_rows // half_rows, across, half_rows, block_cols, model_width)
        return shaped.transpose(0, 2, 1, 3, 4).reshape(total_rows, total_cols, model_width)
    attended = untile(tiles[0])
    grad_queries = untile(tiles[1])
    grad_keys = key_grad[RAD:-RAD, RAD:-RAD].astype(jnp.bfloat16)
    grad_values = value_grad[RAD:-RAD, RAD:-RAD].astype(jnp.bfloat16)
    grad_out_weight = jnp.dot(attended.reshape(-1, model_width).T, grad_out.reshape(-1, model_width), preferred_element_type=jnp.float32).astype(jnp.bfloat16)
    grad_bias = fold_offsets(score_total, offsets, KS)
    return (grad_queries, grad_keys, grad_values, grad_out_weight, grad_bias)
```

```python
import functools
import math

import jax
import jax.numpy as jnp
import numpy as np
from jax import lax
from jax.experimental import pallas as pl
from jax.experimental.pallas import tpu as pltpu
from jax.sharding import PartitionSpec as P

MESH = pl.DeviceIdType.MESH
BF = jnp.bfloat16
F32 = jnp.float32

RAD = 5
KS = 11
D = 1024
HEADS = 16
CH = 16
CW = 8
CELLS = CH * CW
XLO, NY, NZ, XHI, CORES = 2, 4, 8, 2, 2
NX = XLO * XHI
GROUP = NY * CORES
RING = NX * NZ
BLOCKS = 4
BROWS = CH // BLOCKS
BQ = BROWS * CW
MIDK = (BROWS + 2 * RAD) * CW
SIDEK = 72
KEYS = MIDK + 2 * SIDEK
STAGE = 144
EXT = CH + 2 * RAD
FEATS = D // NY
OUTS = D // CORES
PROWS = 16
PCOLS = 256
PIECES = FEATS // PROWS
NEG = -1e30
NEIGHBOURS = ((0, -1), (0, 1), (-1, 0), (1, 0), (-1, -1), (1, -1), (-1, 1), (1, 1))


def key_places():
    rows = np.full(KEYS, 1000, np.int64)
    cols = np.full(KEYS, 1000, np.int64)
    mid = np.arange(MIDK)
    rows[:MIDK], cols[:MIDK] = mid // CW, mid % CW
    side = np.arange(70)
    for first, base in ((MIDK, -RAD), (MIDK + SIDEK, CW)):
        rows[first + 1 : first + 71] = side // RAD
        cols[first + 1 : first + 71] = base + side % RAD
    return rows, cols


def tables():
    rows, cols = key_places()
    query = np.arange(BQ)
    dr = rows[None, :] - RAD - (query // CW)[:, None]
    dc = cols[None, :] - (query % CW)[:, None]
    inside = (np.abs(dr) <= RAD) & (np.abs(dc) <= RAD)
    offsets = np.where(inside, (dr + RAD) * KS + dc + RAD, 127)
    one_hot = offsets[:, :, None] == np.arange(128)[None, None, :]
    places = np.zeros((8, KEYS), np.int32)
    places[0], places[1] = rows, cols
    pack = np.zeros((2 * 80, CELLS), bool)
    edge = np.arange(80)
    pack[edge, edge // RAD * CW + edge % RAD] = True
    pack[80 + edge, edge // RAD * CW + CW - RAD + edge % RAD] = True
    spread = np.zeros((BLOCKS * SIDEK, STAGE), bool)
    for b in range(BLOCKS):
        place = np.arange(SIDEK)
        spread[b * SIDEK + place, 6 + 20 * b + place] = True
    entry = np.arange(STAGE)
    cell = np.where(entry < 32, entry, np.where(entry < 112, entry - 32, entry - 64))
    home = np.zeros((CELLS, 2 * STAGE), bool)
    home[cell // RAD * CW + cell % RAD, entry] = True
    home[cell // RAD * CW + CW - RAD + cell % RAD, STAGE + entry] = True
    heads = np.repeat(np.arange(4), BQ)[:, None] == (np.arange(256) // 64)[None, :]
    as_low = lambda t: np.asarray(t, np.float32).astype(jnp.bfloat16)
    return (as_low(one_hot), places, as_low(pack), as_low(spread), as_low(home), as_low(heads))


def dot(a, b, dims):
    return lax.dot_general(a, b, ((dims[0], dims[1]), ((), ())), preferred_element_type=F32)


NN = ((1,), (0,))
NT = ((1,), (1,))
TN = ((0,), (0,))


def kernel(
    q_hbm, k_hbm, v_hbm, g_hbm, w_hbm, bias_ref, oh_hbm, places_ref, pack_ref, spread_ref, home_ref, heads_ref,
    gq_ref, gk_ref, gv_ref, ow_hbm, ob_ref,
    qv, gv, wv, ohv, mid, panel_l, panel_r, stage_l, stage_r, ga, kb, vb, table, probs, att, att_t, at, go,
    sg_sum, acc_mid, acc_l, acc_r, ret_l, ret_r, rcv_l, rcv_r, up_out, down_out, up_in, down_in,
    wt, rs, out, bias_a, bias_ain, bias_xin, bias_b, bias_zin, bias_c, bias_d,
    loc_sem, halo_ss, halo_rs, go_ss, go_rs, at_ss, at_rs, ret_ss, ret_rs, rs_ss, rs_rs, ag_ss, ag_rs,
    y_ss, y_rs, c_ss, c_rs, ba_ss, ba_rs, bx_ss, bx_rs, bz_ss, bz_rs, bd_ss, bd_rs,
):
    row, col = lax.axis_index("row"), lax.axis_index("col")
    nrow, ncol = XLO * NY, NZ * XHI * CORES
    x = (col // CORES) % XHI * XLO + row // NY
    y, z, core = row % NY, col // (XHI * CORES), col % CORES
    scale = 1.0 / math.sqrt(D // HEADS)

    def device(x_at, y_at, z_at, core_at):
        return (x_at % XLO * NY + y_at, (z_at * XHI + x_at // XLO) * CORES + core_at)

    def neighbour(dr, dc):
        return ((row + dr + nrow) % nrow, (col + dc + ncol) % ncol)

    def member(k):
        yy = (y + k // CORES) % NY
        cc = (core + k % CORES) % CORES
        return yy, cc, device(x, yy, z, cc)

    def on_ring(k):
        xx = (x + k // NZ) % NX
        zz = (z + k % NZ) % NZ
        return xx * NZ + zz, device(xx, y, zz, core)

    me_group = y * CORES + core
    me_ring = x * NZ + z

    def local(src, dst, at_sem):
        return pltpu.make_async_copy(src, dst, loc_sem.at[at_sem])

    def remote(src, dst, ss, rsem, to):
        return pltpu.make_async_remote_copy(
            src_ref=src, dst_ref=dst, send_sem=ss, recv_sem=rsem, device_id=to, device_id_type=MESH
        )

    loads = [
        local(k_hbm, mid.at[0, RAD : RAD + CH], 0),
        local(v_hbm, mid.at[1, RAD : RAD + CH], 1),
        local(g_hbm, gv, 2),
        local(w_hbm, wv, 3),
        local(q_hbm, qv, 4),
        local(oh_hbm, ohv, 5),
    ]
    for c in loads:
        c.start()
    barrier = pltpu.get_barrier_semaphore()
    for dr, dc in NEIGHBOURS:
        pl.semaphore_signal(barrier, inc=1, device_id=neighbour(dr, dc), device_id_type=MESH)

    @pl.loop(1, GROUP)
    def _(k):
        pl.semaphore_signal(barrier, inc=1, device_id=member(k)[2], device_id_type=MESH)

    @pl.loop(1, RING)
    def _(k):
        pl.semaphore_signal(barrier, inc=1, device_id=on_ring(k)[1], device_id_type=MESH)

    loads[0].wait()
    loads[1].wait()
    for i in range(2):
        own = mid[i, RAD : RAD + CH].reshape(CELLS, D)
        packed = dot(pack_ref[...], own, NN).astype(BF)
        panel_l[i] = packed[:80]
        panel_r[i] = packed[80:]
    pl.semaphore_wait(barrier, len(NEIGHBOURS) + GROUP - 1 + RING - 1)

    halo_parts = (
        (panel_l, stage_r.at[:, 32:112]),
        (panel_r, stage_l.at[:, 32:112]),
        (mid.at[:, RAD : 2 * RAD], mid.at[:, RAD + CH :]),
        (mid.at[:, CH : CH + RAD], mid.at[:, :RAD]),
        (panel_l.at[:, 0:32], stage_r.at[:, 112:144]),
        (panel_l.at[:, 48:80], stage_r.at[:, 0:32]),
        (panel_r.at[:, 0:32], stage_l.at[:, 112:144]),
        (panel_r.at[:, 48:80], stage_l.at[:, 0:32]),
    )
    halo = [
        remote(src, dst, halo_ss.at[i], halo_rs.at[i], neighbour(*NEIGHBOURS[i]))
        for i, (src, dst) in enumerate(halo_parts)
    ]
    for c in halo:
        c.start()

    loads[2].wait()

    def go_copy(k):
        yy, cc, to = member(k)
        lanes = pl.ds(pl.multiple_of(cc * OUTS, OUTS), OUTS)
        return remote(gv.at[:, :, lanes], go.at[me_group], go_ss.at[k], go_rs.at[k], to)

    @pl.loop(1, GROUP)
    def _(k):
        go_copy(k).start()

    own_lanes = pl.ds(pl.multiple_of(core * OUTS, OUTS), OUTS)
    go_own = local(gv.at[:, :, own_lanes], go.at[me_group], 6)
    go_own.start()

    loads[3].wait()
    ga[...] = dot(gv[...].reshape(CELLS, D), wv[...], NT).astype(BF)

    loads[5].wait()
    padded = jnp.concatenate([bias_ref[...], jnp.full((HEADS, 128 - KS * KS), NEG, F32)], axis=1)
    high = padded.astype(BF)
    rest = padded - high.astype(F32)
    middle = rest.astype(BF)
    low = (rest - middle.astype(F32)).astype(BF)
    three = jnp.concatenate([high, middle, low], axis=0)
    for i in range(BQ):
        terms = dot(three, ohv[i], NT)
        table[:, i, :] = terms[:HEADS] + terms[HEADS : 2 * HEADS] + terms[2 * HEADS :]
    for ref in (acc_mid, acc_l, acc_r, sg_sum):
        ref[...] = jnp.zeros_like(ref)

    loads[4].wait()
    for c in halo:
        c.wait()
    for i, slab in enumerate((kb, vb)):
        left = dot(spread_ref[...], stage_l[i], NN)
        right = dot(spread_ref[...], stage_r[i], NN)
        for b in range(BLOCKS):
            slab[b, :MIDK] = mid[i, b * BROWS : b * BROWS + BROWS + 2 * RAD].reshape(MIDK, D)
            rows = slice(b * SIDEK, (b + 1) * SIDEK)
            slab[b, MIDK:] = jnp.concatenate([left[rows], right[rows]], axis=0).astype(BF)

    mask_low = heads_ref[...]
    mask_wide = mask_low.astype(F32)

    def spread_heads(tile):
        return jnp.concatenate([tile] * 4, axis=0) * mask_low

    def fold_heads(full):
        return jnp.sum((full * mask_wide).reshape(4, BQ, 256), axis=0)

    key_row, key_col = places_ref[0:1, :], places_ref[1:2, :]
    grid_col = col * CW + key_col
    col_ok = (grid_col >= 0) & (grid_col < ncol * CW)
    q2 = qv[...].reshape(CELLS, D)
    for b in range(BLOCKS):
        cells = slice(b * BQ, (b + 1) * BQ)
        grid_row = row * CH + b * BROWS - RAD + key_row
        present = col_ok & (grid_row >= 0) & (grid_row < nrow * CH)
        absent = jnp.where(present, 0.0, NEG)
        for h in range(4):
            lanes = slice(h * 256, (h + 1) * 256)
            qm = spread_heads(q2[cells, lanes])
            bias = table[4 * h : 4 * h + 4].reshape(4 * BQ, KEYS)
            scores = dot(qm, kb[b, :, lanes], NT) * scale + bias + absent
            weights = jnp.exp(scores - jnp.max(scores, axis=1, keepdims=True))
            p = weights * (1.0 / jnp.sum(weights, axis=1, keepdims=True))
            probs[b * 4 + h] = p
            att[cells, lanes] = fold_heads(dot(p.astype(BF), vb[b, :, lanes], NN)).astype(BF)
    att_t[...] = att[...].T

    def at_copy(k):
        yy, cc, to = member(k)
        src = att_t.at[pl.ds(pl.multiple_of(yy * FEATS, FEATS), FEATS)]
        dst = at.at[:, pl.ds(pl.multiple_of(me_group * CELLS, CELLS), CELLS)]
        return remote(src, dst, at_ss.at[k], at_rs.at[k], to)

    @pl.loop(1, GROUP)
    def _(k):
        at_copy(k).start()

    at_own = local(
        att_t.at[pl.ds(pl.multiple_of(y * FEATS, FEATS), FEATS)],
        at.at[:, pl.ds(pl.multiple_of(me_group * CELLS, CELLS), CELLS)],
        7,
    )
    at_own.start()

    for b in range(BLOCKS):
        cells = slice(b * BQ, (b + 1) * BQ)
        for h in range(4):
            lanes = slice(h * 256, (h + 1) * 256)
            qm = spread_heads(q2[cells, lanes])
            gm = spread_heads(ga[cells, lanes])
            p = probs[b * 4 + h]
            dp = dot(gm, vb[b, :, lanes], NT)
            sg = p * (dp - jnp.sum(p * dp, axis=1, keepdims=True))
            sg_sum[4 * h : 4 * h + 4] += sg.reshape(4, BQ, KEYS)
            sl = sg.astype(BF)
            gq_ref[cells, lanes] = (fold_heads(dot(sl, kb[b, :, lanes], NN)) * scale).astype(BF)
            parts = (dot(sl, qm, TN) * scale, dot(p.astype(BF), gm, TN))
            for i, part in enumerate(parts):
                acc_mid[i, b * BQ : b * BQ + MIDK, lanes] += part[:MIDK]
                acc_l[i, 6 + 20 * b : 6 + 20 * b + SIDEK, lanes] += part[MIDK : MIDK + SIDEK]
                acc_r[i, 6 + 20 * b : 6 + 20 * b + SIDEK, lanes] += part[MIDK + SIDEK :]

    ret_l[...] = acc_l[...].astype(BF)
    ret_r[...] = acc_r[...].astype(BF)
    up_out[...] = acc_mid[:, : RAD * CW].reshape(2, RAD, CW, D).astype(BF)
    down_out[...] = acc_mid[:, (RAD + CH) * CW :].reshape(2, RAD, CW, D).astype(BF)
    ret_parts = (
        (ret_l.at[:, 32:112], rcv_r.at[:, 32:112]),
        (ret_r.at[:, 32:112], rcv_l.at[:, 32:112]),
        (up_out, down_in),
        (down_out, up_in),
        (ret_l.at[:, 0:32], rcv_r.at[:, 112:144]),
        (ret_l.at[:, 112:144], rcv_r.at[:, 0:32]),
        (ret_r.at[:, 0:32], rcv_l.at[:, 112:144]),
        (ret_r.at[:, 112:144], rcv_l.at[:, 0:32]),
    )
    ret = [
        remote(src, dst, ret_ss.at[i], ret_rs.at[i], neighbour(*NEIGHBOURS[i]))
        for i, (src, dst) in enumerate(ret_parts)
    ]
    for c in ret:
        c.start()

    bias_sum = jnp.zeros((2 * HEADS, 128), F32)
    for i in range(BQ):
        sums = sg_sum[:, i, :]
        high = sums.astype(BF)
        low = (sums - high.astype(F32)).astype(BF)
        bias_sum = bias_sum + dot(jnp.concatenate([high, low], axis=0), ohv[i], NN)
    bias_sum = bias_sum[:HEADS] + bias_sum[HEADS:]
    per = HEADS // GROUP
    bias_a[...] = jnp.zeros_like(bias_a)
    for i in range(GROUP):
        bias_a[i, :per] = bias_sum[i * per : (i + 1) * per]

    def ba_copy(k):
        yy, cc, to = member(k)
        return remote(bias_a.at[yy * CORES + cc], bias_ain.at[k], ba_ss.at[k], ba_rs.at[k], to)

    @pl.loop(1, GROUP)
    def _(k):
        ba_copy(k).start()

    go_own.wait()
    at_own.wait()

    @pl.loop(1, GROUP)
    def _(k):
        go_copy(k).wait()
        at_copy(k).wait()

    wt[...] = dot(at[...], go[...].reshape(GROUP * CELLS, OUTS), NN).reshape(PIECES, PROWS, OUTS).astype(BF)

    def piece(ref, n, base_row=0, base_col=0):
        lanes = pl.ds(pl.multiple_of(base_col + n % 2 * PCOLS, PCOLS), PCOLS)
        return ref.at[base_row + n // 2, :, lanes]

    def rs_copy(k):
        n, to = on_ring(k)
        return remote(piece(wt, n), rs.at[k], rs_ss.at[k], rs_rs.at[k], to)

    @pl.loop(1, RING)
    def _(k):
        rs_copy(k).start()

    rs_own = local(piece(wt, me_ring), rs.at[0], 8)
    rs_own.start()

    @pl.loop(1, GROUP)
    def _(k):
        ba_copy(k).wait()

    bias_ain[0] = bias_a[me_group]
    bias_b[0] = jnp.sum(bias_ain[...], axis=0)

    def bx_copy(k):
        return remote(
            bias_b.at[0], bias_xin.at[k], bx_ss.at[k], bx_rs.at[k], device((x + k) % NX, y, z, core)
        )

    def bz_copy(k):
        return remote(
            bias_b.at[1], bias_zin.at[k], bz_ss.at[k], bz_rs.at[k], device(x, y, (z + k) % NZ, core)
        )

    @pl.loop(1, NX)
    def _(k):
        bx_copy(k).start()

    rs_own.wait()

    @pl.loop(1, RING)
    def _(k):
        rs_copy(k).wait()

    total = jnp.sum(rs[...].astype(F32), axis=0)
    wt_final = total.astype(BF)
    out[y * (PIECES) + me_ring // 2, :, pl.ds(pl.multiple_of(core * OUTS + me_ring % 2 * PCOLS, PCOLS), PCOLS)] = wt_final
    mine = piece(out, me_ring, y * PIECES, core * OUTS)

    def ag_copy(k):
        return remote(mine, mine, ag_ss.at[k], ag_rs.at[k], on_ring(k)[1])

    @pl.loop(1, RING)
    def _(k):
        ag_copy(k).start()

    @pl.loop(1, NX)
    def _(k):
        bx_copy(k).wait()

    bias_xin[0] = bias_b[0]
    bias_b[1] = jnp.sum(bias_xin[...], axis=0)

    @pl.loop(1, NZ)
    def _(k):
        bz_copy(k).start()

    for c in ret:
        c.wait()
    home = home_ref[...]
    for i, ref in enumerate((gk_ref, gv_ref)):
        back = jnp.concatenate([rcv_l[i], rcv_r[i]], axis=0)
        total = acc_mid[i, RAD * CW : (RAD + CH) * CW] + dot(home, back, NN)
        gap = jnp.zeros((CELLS - RAD * CW, D), F32)
        above = up_in[i].astype(F32).reshape(RAD * CW, D)
        below = down_in[i].astype(F32).reshape(RAD * CW, D)
        total = total + jnp.concatenate([above, gap], axis=0) + jnp.concatenate([gap, below], axis=0)
        ref[...] = total.astype(BF)

    @pl.loop(1, RING)
    def _(k):
        ag_copy(k).wait()

    quarter = out.at[pl.ds(y * PIECES, PIECES), :, own_lanes]

    def y_copy(k):
        return remote(quarter, quarter, y_ss.at[k], y_rs.at[k], device(x, (y + k) % NY, z, core))

    @pl.loop(1, NY)
    def _(k):
        y_copy(k).start()

    def c_copy(k):
        part = out.at[pl.ds((y + NY - k) % NY * PIECES, PIECES), :, own_lanes]
        return remote(part, part, c_ss.at[k], c_rs.at[k], device(x, y, z, 1 - core))

    c_copy(0).start()

    @pl.loop(1, NZ)
    def _(k):
        bz_copy(k).wait()

    bias_zin[0] = bias_b[1]
    bias_c[me_group] = jnp.sum(bias_zin[...], axis=0)
    bias_mine = bias_c.at[me_group]

    def bd_copy(k):
        return remote(bias_mine, bias_mine, bd_ss.at[k], bd_rs.at[k], member(k)[2])

    @pl.loop(1, GROUP)
    def _(k):
        bd_copy(k).start()

    @pl.loop(1, NY)
    def _(k):
        y_copy(k).wait()
        c_copy(k).start()

    @pl.loop(1, GROUP)
    def _(k):
        bd_copy(k).wait()

    ob_ref[...] = jnp.concatenate([bias_c[i, :per, : KS * KS] for i in range(GROUP)], axis=0)

    @pl.loop(0, NY)
    def _(k):
        c_copy(k).wait()

    store = local(out, ow_hbm, 9)
    store.start()
    store.wait()


def on_device(queries, keys, values, grad_out, out_weight, rel_bias):
    one_hot, places, pack, spread, home, heads = tables()
    cells_out = jax.ShapeDtypeStruct((CELLS, D), BF)
    dma = pltpu.SemaphoreType.DMA
    vm = pltpu.VMEM
    in_hbm = pl.BlockSpec(memory_space=pl.ANY)
    in_vmem = pl.BlockSpec(memory_space=pltpu.VMEM)
    scratch = [
        vm((CH, CW, D), BF),
        vm((CH, CW, D), BF),
        vm((D, D), BF),
        vm((BQ, KEYS, 128), BF),
        vm((2, EXT, CW, D), BF),
        vm((2, 80, D), BF),
        vm((2, 80, D), BF),
        vm((2, STAGE, D), BF),
        vm((2, STAGE, D), BF),
        vm((CELLS, D), BF),
        vm((BLOCKS, KEYS, D), BF),
        vm((BLOCKS, KEYS, D), BF),
        vm((HEADS, BQ, KEYS), F32),
        vm((16, 4 * BQ, KEYS), F32),
        vm((CELLS, D), BF),
        vm((D, CELLS), BF),
        vm((FEATS, GROUP * CELLS), BF),
        vm((GROUP, CH, CW, OUTS), BF),
        vm((HEADS, BQ, KEYS), F32),
        vm((2, EXT * CW, D), F32),
        vm((2, STAGE, D), F32),
        vm((2, STAGE, D), F32),
        vm((2, STAGE, D), BF),
        vm((2, STAGE, D), BF),
        vm((2, STAGE, D), BF),
        vm((2, STAGE, D), BF),
        vm((2, RAD, CW, D), BF),
        vm((2, RAD, CW, D), BF),
        vm((2, RAD, CW, D), BF),
        vm((2, RAD, CW, D), BF),
        vm((PIECES, PROWS, OUTS), BF),
        vm((RING, PROWS, PCOLS), BF),
        vm((D // PROWS, PROWS, D), BF),
        vm((GROUP, 8, 128), F32),
        vm((GROUP, 8, 128), F32),
        vm((NX, 8, 128), F32),
        vm((2, 8, 128), F32),
        vm((NZ, 8, 128), F32),
        vm((GROUP, 8, 128), F32),
        vm((GROUP, 8, 128), F32),
        dma((10,)),
    ]
    for count in (8, GROUP, GROUP, 8, RING, RING, NY, NY, GROUP, NX, NZ, GROUP):
        scratch += [dma((count,)), dma((count,))]
    results = pl.pallas_call(
        kernel,
        out_shape=(
            cells_out,
            cells_out,
            cells_out,
            jax.ShapeDtypeStruct((D // PROWS, PROWS, D), BF),
            jax.ShapeDtypeStruct((HEADS, KS * KS), F32),
        ),
        in_specs=[in_hbm] * 5 + [in_vmem, in_hbm] + [in_vmem] * 5,
        out_specs=(in_vmem, in_vmem, in_vmem, in_hbm, in_vmem),
        scratch_shapes=scratch,
        compiler_params=pltpu.CompilerParams(
            collective_id=0, has_side_effects=True, vmem_limit_bytes=56 * 2**20
        ),
        cost_estimate=pl.CostEstimate(flops=3 * 10**9, bytes_accessed=8 * 2**20, transcendentals=10**6),
        name="attention_backward",
    )(queries, keys, values, grad_out, out_weight, rel_bias, one_hot, places, pack, spread, home, heads)
    gq, gk, gv, gw, gb = results
    shape = queries.shape
    return gq.reshape(shape), gk.reshape(shape), gv.reshape(shape), gw.reshape(D, D), gb


def solution(mesh):
    cells = P("row", "col", None)
    return jax.shard_map(
        on_device,
        mesh=mesh,
        in_specs=(cells, cells, cells, cells, P(), P()),
        out_specs=(cells, cells, cells, P(), P()),
        check_vma=False,
    )
```

```python
import functools
import math

import jax
import jax.numpy as jnp
import numpy as np
from jax import lax
from jax.experimental import pallas as pl
from jax.experimental.pallas import tpu as pltpu
from jax.sharding import PartitionSpec as P

MESH = pl.DeviceIdType.MESH
BF = jnp.bfloat16
F32 = jnp.float32

RAD = 5
KS = 11
D = 1024
HEADS = 16
CH = 16
CW = 8
CELLS = CH * CW
XLO, NY, NZ, XHI, CORES = 2, 4, 8, 2, 2
NX = XLO * XHI
GROUP = NY * CORES
BLOCKS = 4
BROWS = CH // BLOCKS
BQ = BROWS * CW
MIDK = (BROWS + 2 * RAD) * CW
SIDEK = 72
KEYS = MIDK + 2 * SIDEK
STAGE = 144
EXT = CH + 2 * RAD
FEATS = D // NY
OUTS = D // CORES
PROWS = 16
XPIECES = FEATS // PROWS // NX
NEG = -1e30
NEIGHBOURS = ((0, -1), (0, 1), (-1, 0), (1, 0), (-1, -1), (1, -1), (-1, 1), (1, 1))


def key_places():
    rows = np.full(KEYS, 1000, np.int64)
    cols = np.full(KEYS, 1000, np.int64)
    mid = np.arange(MIDK)
    rows[:MIDK], cols[:MIDK] = mid // CW, mid % CW
    side = np.arange(70)
    for first, base in ((MIDK, -RAD), (MIDK + SIDEK, CW)):
        rows[first + 1 : first + 71] = side // RAD
        cols[first + 1 : first + 71] = base + side % RAD
    return rows, cols


def tables():
    rows, cols = key_places()
    query = np.arange(BQ)
    dr = rows[None, :] - RAD - (query // CW)[:, None]
    dc = cols[None, :] - (query % CW)[:, None]
    inside = (np.abs(dr) <= RAD) & (np.abs(dc) <= RAD)
    offsets = np.where(inside, (dr + RAD) * KS + dc + RAD, 127)
    one_hot = offsets[:, :, None] == np.arange(128)[None, None, :]
    places = np.zeros((8, KEYS), np.int32)
    places[0], places[1] = rows, cols
    pack = np.zeros((2 * 80, CELLS), bool)
    edge = np.arange(80)
    pack[edge, edge // RAD * CW + edge % RAD] = True
    pack[80 + edge, edge // RAD * CW + CW - RAD + edge % RAD] = True
    spread = np.zeros((BLOCKS * SIDEK, STAGE), bool)
    for b in range(BLOCKS):
        place = np.arange(SIDEK)
        spread[b * SIDEK + place, 6 + 20 * b + place] = True
    join = np.zeros((2 * STAGE, BLOCKS * 2 * SIDEK), bool)
    for b in range(BLOCKS):
        place = np.arange(SIDEK)
        join[6 + 20 * b + place, 2 * SIDEK * b + place] = True
        join[STAGE + 6 + 20 * b + place, 2 * SIDEK * b + SIDEK + place] = True
    entry = np.arange(STAGE)
    cell = np.where(entry < 32, entry, np.where(entry < 112, entry - 32, entry - 64))
    home = np.zeros((CELLS, 2 * STAGE), bool)
    home[cell // RAD * CW + cell % RAD, entry] = True
    home[cell // RAD * CW + CW - RAD + cell % RAD, STAGE + entry] = True
    heads = np.repeat(np.arange(4), BQ)[:, None] == (np.arange(256) // 64)[None, :]
    as_low = lambda t: np.asarray(t, np.float32).astype(jnp.bfloat16)
    return (as_low(one_hot), places, as_low(pack), as_low(spread), as_low(join), as_low(home), as_low(heads))


def dot(a, b, dims):
    return lax.dot_general(a, b, ((dims[0], dims[1]), ((), ())), preferred_element_type=F32)


NN = ((1,), (0,))
NT = ((1,), (1,))
TN = ((0,), (0,))


def kernel(
    q_hbm, k_hbm, v_hbm, g_hbm, w_hbm, bias_ref, oh_hbm, places_ref, pack_ref, spread_ref, join_ref, home_ref, heads_ref,
    gq_hbm, gk_hbm, gv_hbm, ow_hbm, ob_ref,
    qv, gv, wv, ohv, mid, panel_l, panel_r, stage_l, stage_r, ga, kb, vb, table, probs, att, at, go,
    sg_sum, acc_mid, side, ret_l, ret_r, rcv_l, rcv_r, up_out, down_out, up_in, down_in,
    gq, gk, gval, wt, rx, wz, rz, out, bias_a, bias_ain, bias_xin, bias_b, bias_zin, bias_c,
    loc_sem, halo_ss, halo_rs, go_ss, go_rs, at_ss, at_rs, ret_ss, ret_rs, rx_ss, rx_rs, rz_ss, rz_rs, zg_ss, zg_rs,
    a2_ss, a2_rs, b2_ss, b2_rs, a3_ss, a3_rs, b3_ss, b3_rs, ca_ss, ca_rs, cb_ss, cb_rs,
    ba_ss, ba_rs, bx_ss, bx_rs, bz_ss, bz_rs, bd_ss, bd_rs,
):
    row, col = lax.axis_index("row"), lax.axis_index("col")
    nrow, ncol = XLO * NY, NZ * XHI * CORES
    x = (col // CORES) % XHI * XLO + row // NY
    y, z, core = row % NY, col // (XHI * CORES), col % CORES
    scale = 1.0 / math.sqrt(D // HEADS)

    def device(x_at, y_at, z_at, core_at):
        return (x_at % XLO * NY + y_at, (z_at * XHI + x_at // XLO) * CORES + core_at)

    def neighbour(dr, dc):
        return ((row + dr + nrow) % nrow, (col + dc + ncol) % ncol)

    def member(k):
        yy = (y + k // CORES) % NY
        cc = (core + k % CORES) % CORES
        return yy, cc, device(x, yy, z, cc)

    def along_x(k):
        return device((x + k) % NX, y, z, core)

    def along_y(k):
        return device(x, (y + k) % NY, z, core)

    def along_z(k):
        return device(x, y, (z + k) % NZ, core)

    me_group = y * CORES + core

    def local(src, dst, at_sem):
        return pltpu.make_async_copy(src, dst, loc_sem.at[at_sem])

    def remote(src, dst, ss, rsem, to):
        return pltpu.make_async_remote_copy(
            src_ref=src, dst_ref=dst, send_sem=ss, recv_sem=rsem, device_id=to, device_id_type=MESH
        )

    loads = [
        local(k_hbm, mid.at[0, RAD : RAD + CH], 0),
        local(v_hbm, mid.at[1, RAD : RAD + CH], 1),
        local(g_hbm, gv, 2),
        local(w_hbm, wv, 3),
        local(q_hbm, qv, 4),
        local(oh_hbm, ohv, 5),
    ]
    for c in loads:
        c.start()
    barrier = pltpu.get_barrier_semaphore()
    for dr, dc in NEIGHBOURS:
        pl.semaphore_signal(barrier, inc=1, device_id=neighbour(dr, dc), device_id_type=MESH)

    @pl.loop(1, GROUP)
    def _(k):
        pl.semaphore_signal(barrier, inc=1, device_id=member(k)[2], device_id_type=MESH)

    @pl.loop(1, NX)
    def _(k):
        pl.semaphore_signal(barrier, inc=1, device_id=along_x(k), device_id_type=MESH)

    @pl.loop(1, NZ)
    def _(k):
        pl.semaphore_signal(barrier, inc=1, device_id=along_z(k), device_id_type=MESH)

    loads[0].wait()
    loads[1].wait()
    for i in range(2):
        own = mid[i, RAD : RAD + CH].reshape(CELLS, D)
        packed = dot(pack_ref[...], own, NN).astype(BF)
        panel_l[i] = packed[:80]
        panel_r[i] = packed[80:]
    pl.semaphore_wait(barrier, len(NEIGHBOURS) + GROUP - 1 + NX - 1 + NZ - 1)

    halo_parts = (
        (panel_l, stage_r.at[:, 32:112]),
        (panel_r, stage_l.at[:, 32:112]),
        (mid.at[:, RAD : 2 * RAD], mid.at[:, RAD + CH :]),
        (mid.at[:, CH : CH + RAD], mid.at[:, :RAD]),
        (panel_l.at[:, 0:32], stage_r.at[:, 112:144]),
        (panel_l.at[:, 48:80], stage_r.at[:, 0:32]),
        (panel_r.at[:, 0:32], stage_l.at[:, 112:144]),
        (panel_r.at[:, 48:80], stage_l.at[:, 0:32]),
    )
    halo = [
        remote(src, dst, halo_ss.at[i], halo_rs.at[i], neighbour(*NEIGHBOURS[i]))
        for i, (src, dst) in enumerate(halo_parts)
    ]
    for c in halo:
        c.start()

    loads[2].wait()

    def go_copy(k):
        yy, cc, to = member(k)
        lanes = pl.ds(pl.multiple_of(cc * OUTS, OUTS), OUTS)
        return remote(gv.at[:, :, lanes], go.at[me_group], go_ss.at[k], go_rs.at[k], to)

    @pl.loop(1, GROUP)
    def _(k):
        go_copy(k).start()

    own_lanes = pl.ds(pl.multiple_of(core * OUTS, OUTS), OUTS)
    go_own = local(gv.at[:, :, own_lanes], go.at[me_group], 6)
    go_own.start()

    loads[3].wait()
    ga[...] = dot(gv[...].reshape(CELLS, D), wv[...], NT).astype(BF)

    loads[5].wait()
    padded = jnp.concatenate([bias_ref[...], jnp.full((HEADS, 128 - KS * KS), NEG, F32)], axis=1)
    high = padded.astype(BF)
    rest = padded - high.astype(F32)
    middle = rest.astype(BF)
    low = (rest - middle.astype(F32)).astype(BF)
    three = jnp.concatenate([high, middle, low], axis=0)
    for i in range(BQ):
        terms = dot(three, ohv[i], NT)
        table[:, i, :] = terms[:HEADS] + terms[HEADS : 2 * HEADS] + terms[2 * HEADS :]
    for ref in (acc_mid, sg_sum):
        ref[...] = jnp.zeros_like(ref)

    loads[4].wait()
    halo[2].wait()
    halo[3].wait()
    for i, slab in enumerate((kb, vb)):
        for b in range(BLOCKS):
            slab[b, :MIDK] = mid[i, b * BROWS : b * BROWS + BROWS + 2 * RAD].reshape(MIDK, D)
    for i in (0, 1, 4, 5, 6, 7):
        halo[i].wait()
    for i, slab in enumerate((kb, vb)):
        left = dot(spread_ref[...], stage_l[i], NN)
        right = dot(spread_ref[...], stage_r[i], NN)
        for b in range(BLOCKS):
            rows = slice(b * SIDEK, (b + 1) * SIDEK)
            slab[b, MIDK:] = jnp.concatenate([left[rows], right[rows]], axis=0).astype(BF)

    mask_low = heads_ref[...]
    mask_wide = mask_low.astype(F32)

    def spread_heads(tile):
        return jnp.concatenate([tile] * 4, axis=0) * mask_low

    def fold_heads(full):
        return jnp.sum((full * mask_wide).reshape(4, BQ, 256), axis=0)

    key_row, key_col = places_ref[0:1, :], places_ref[1:2, :]
    grid_col = col * CW + key_col
    col_ok = (grid_col >= 0) & (grid_col < ncol * CW)
    q2 = qv[...].reshape(CELLS, D)
    groups = [slice(h * 256, (h + 1) * 256) for h in range(4)]

    def forward(b):
        cells = slice(b * BQ, (b + 1) * BQ)
        grid_row = row * CH + b * BROWS - RAD + key_row
        present = col_ok & (grid_row >= 0) & (grid_row < nrow * CH)
        absent = jnp.where(present, 0.0, NEG)
        scores = [dot(spread_heads(q2[cells, n]), kb[b, :, n], NT) for n in groups]
        scores = [
            s * scale + (table[4 * h : 4 * h + 4].reshape(4 * BQ, KEYS) + absent) for h, s in enumerate(scores)
        ]
        weights = [jnp.exp(s - jnp.max(s, axis=1, keepdims=True)) for s in scores]
        p = [e * (1.0 / jnp.sum(e, axis=1, keepdims=True)) for e in weights]
        for h in range(4):
            probs[b * 4 + h] = p[h]
        full = [dot(t.astype(BF), vb[b, :, n], NN) for t, n in zip(p, groups)]
        for t, n in zip(full, groups):
            att[cells, n] = fold_heads(t).astype(BF)

    half_cells = CELLS // 2

    def at_copy(part, k):
        yy, cc, to = member(k)
        src = att.at[pl.ds(part * half_cells, half_cells), pl.ds(pl.multiple_of(yy * FEATS, FEATS), FEATS)]
        dst = at.at[me_group, pl.ds(part * half_cells, half_cells)]
        return remote(src, dst, at_ss.at[part, k], at_rs.at[part, k], to)

    for part in range(2):
        forward(2 * part)
        forward(2 * part + 1)

        @pl.loop(1, GROUP)
        def _(k):
            at_copy(part, k).start()

    at_own = local(att.at[:, pl.ds(pl.multiple_of(y * FEATS, FEATS), FEATS)], at.at[me_group], 7)
    at_own.start()

    def backward(b):
        cells = slice(b * BQ, (b + 1) * BQ)
        qm = [spread_heads(q2[cells, n]) for n in groups]
        gm = [spread_heads(ga[cells, n]) for n in groups]
        p = [probs[b * 4 + h] for h in range(4)]
        dp = [dot(g, vb[b, :, n], NT) for g, n in zip(gm, groups)]
        sg = [t * (d - jnp.sum(t * d, axis=1, keepdims=True)) for t, d in zip(p, dp)]
        for h in range(4):
            sg_sum[4 * h : 4 * h + 4] += sg[h].reshape(4, BQ, KEYS)
        sl = [t.astype(BF) for t in sg]
        for h, n in enumerate(groups):
            gq[cells, n] = (fold_heads(dot(sl[h], kb[b, :, n], NN)) * scale).astype(BF)
            parts = (dot(sl[h], qm[h], TN) * scale, dot(p[h].astype(BF), gm[h], TN))
            for i, part in enumerate(parts):
                acc_mid[i, b * BQ : b * BQ + MIDK, n] += part[:MIDK]
                side[i, b * 2 * SIDEK : (b + 1) * 2 * SIDEK, n] = part[MIDK:].astype(BF)

    backward(0)
    backward(1)
    go_own.wait()
    at_own.wait()

    @pl.loop(1, GROUP)
    def _(k):
        go_copy(k).wait()
        at_copy(0, k).wait()
        at_copy(1, k).wait()

    wt[...] = dot(at[...].reshape(GROUP * CELLS, FEATS), go[...].reshape(GROUP * CELLS, OUTS), TN).reshape(FEATS // PROWS, PROWS, OUTS).astype(BF)

    def rx_copy(k):
        part = wt.at[pl.ds((x + k) % NX * XPIECES, XPIECES)]
        return remote(part, rx.at[k], rx_ss.at[k], rx_rs.at[k], along_x(k))

    @pl.loop(1, NX)
    def _(k):
        rx_copy(k).start()

    rx_own = local(wt.at[pl.ds(x * XPIECES, XPIECES)], rx.at[0], 8)
    rx_own.start()
    backward(2)
    backward(3)
    gq_store = local(gq, gq_hbm, 9)
    gq_store.start()

    for i in range(2):
        joined = dot(join_ref[...], side[i], NN).astype(BF)
        ret_l[i] = joined[:STAGE]
        ret_r[i] = joined[STAGE:]
    up_out[...] = acc_mid[:, : RAD * CW].reshape(2, RAD, CW, D).astype(BF)
    down_out[...] = acc_mid[:, (RAD + CH) * CW :].reshape(2, RAD, CW, D).astype(BF)
    ret_parts = (
        (ret_l.at[:, 32:112], rcv_r.at[:, 32:112]),
        (ret_r.at[:, 32:112], rcv_l.at[:, 32:112]),
        (up_out, down_in),
        (down_out, up_in),
        (ret_l.at[:, 0:32], rcv_r.at[:, 112:144]),
        (ret_l.at[:, 112:144], rcv_r.at[:, 0:32]),
        (ret_r.at[:, 0:32], rcv_l.at[:, 112:144]),
        (ret_r.at[:, 112:144], rcv_l.at[:, 0:32]),
    )
    ret = [
        remote(src, dst, ret_ss.at[i], ret_rs.at[i], neighbour(*NEIGHBOURS[i]))
        for i, (src, dst) in enumerate(ret_parts)
    ]
    for c in ret:
        c.start()

    rx_own.wait()

    @pl.loop(1, NX)
    def _(k):
        rx_copy(k).wait()

    total = jnp.sum(rx[...].astype(F32), axis=0).astype(BF)
    half = OUTS // 2
    for i in range(XPIECES):
        for j in range(2):
            first, second = total[i, :, j * 128 : j * 128 + 128], total[i, :, half + j * 128 : half + j * 128 + 128]
            wz[2 * i + j] = jnp.concatenate([first, second], axis=1)

    def rz_copy(k):
        return remote(wz.at[(z + k) % NZ], rz.at[k], rz_ss.at[k], rz_rs.at[k], along_z(k))

    @pl.loop(1, NZ)
    def _(k):
        rz_copy(k).start()

    bias_sum = jnp.zeros((2 * HEADS, 128), F32)
    for i in range(BQ):
        sums = sg_sum[:, i, :]
        high = sums.astype(BF)
        low = (sums - high.astype(F32)).astype(BF)
        bias_sum = bias_sum + dot(jnp.concatenate([high, low], axis=0), ohv[i], NN)
    bias_sum = bias_sum[:HEADS] + bias_sum[HEADS:]
    per = HEADS // GROUP
    bias_a[...] = jnp.zeros_like(bias_a)
    for i in range(GROUP):
        bias_a[i, :per] = bias_sum[i * per : (i + 1) * per]

    def ba_copy(k):
        yy, cc, to = member(k)
        return remote(bias_a.at[yy * CORES + cc], bias_ain.at[k], ba_ss.at[k], ba_rs.at[k], to)

    @pl.loop(1, GROUP)
    def _(k):
        ba_copy(k).start()

    rz[0] = wz[z]

    @pl.loop(1, NZ)
    def _(k):
        rz_copy(k).wait()

    final = jnp.sum(rz[...].astype(F32), axis=0).astype(BF)
    spot = x * XPIECES + z // 2
    out[core, 0, y, spot, z % 2] = final[:, :128]
    out[core, 1, y, spot, z % 2] = final[:, 128:]
    mine = out.at[core, :, y, spot, z % 2]

    def zg_copy(k):
        return remote(mine, mine, zg_ss.at[k], zg_rs.at[k], along_z(k))

    @pl.loop(1, NZ)
    def _(k):
        zg_copy(k).start()

    @pl.loop(1, GROUP)
    def _(k):
        ba_copy(k).wait()

    bias_ain[0] = bias_a[me_group]
    bias_b[0] = jnp.sum(bias_ain[...], axis=0)

    def bx_copy(k):
        return remote(bias_b.at[0], bias_xin.at[k], bx_ss.at[k], bx_rs.at[k], along_x(k))

    def bz_copy(k):
        return remote(bias_b.at[1], bias_zin.at[k], bz_ss.at[k], bz_rs.at[k], along_z(k))

    @pl.loop(1, NX)
    def _(k):
        bx_copy(k).start()

    @pl.loop(1, NZ)
    def _(k):
        zg_copy(k).wait()

    slab_a = out.at[core, 0, y, pl.ds(x * XPIECES, XPIECES)]
    slab_b = out.at[core, 1, y, pl.ds(x * XPIECES, XPIECES)]

    def a2_copy(k):
        return remote(slab_a, slab_a, a2_ss.at[k], a2_rs.at[k], along_x(k))

    def b2_copy(k):
        return remote(slab_b, slab_b, b2_ss.at[k], b2_rs.at[k], along_y(k))

    @pl.loop(1, NX)
    def _(k):
        a2_copy(k).start()

    @pl.loop(1, NY)
    def _(k):
        b2_copy(k).start()

    @pl.loop(1, NX)
    def _(k):
        bx_copy(k).wait()

    bias_xin[0] = bias_b[0]
    bias_b[1] = jnp.sum(bias_xin[...], axis=0)

    @pl.loop(1, NZ)
    def _(k):
        bz_copy(k).start()

    def part_a(k):
        return out.at[core, 0, (y + k + NY) % NY]

    def part_b(k):
        return out.at[core, 1, :, pl.ds((x + k + NX) % NX * XPIECES, XPIECES)]

    def a3_copy(k):
        return remote(part_a(0), part_a(0), a3_ss.at[k], a3_rs.at[k], along_y(k))

    def b3_copy(k):
        return remote(part_b(0), part_b(0), b3_ss.at[k], b3_rs.at[k], along_x(k))

    def ca_copy(k):
        return remote(part_a(-k), part_a(-k), ca_ss.at[k], ca_rs.at[k], device(x, y, z, 1 - core))

    def cb_copy(k):
        return remote(part_b(-k), part_b(-k), cb_ss.at[k], cb_rs.at[k], device(x, y, z, 1 - core))

    @pl.loop(1, NX)
    def _(k):
        a2_copy(k).wait()

    @pl.loop(1, NY)
    def _(k):
        a3_copy(k).start()

    @pl.loop(1, NY)
    def _(k):
        b2_copy(k).wait()

    @pl.loop(1, NX)
    def _(k):
        b3_copy(k).start()

    ca_copy(0).start()
    cb_copy(0).start()

    for c in ret:
        c.wait()
    home = home_ref[...]
    grad_stores = []
    for i, (ref, hbm) in enumerate(((gk, gk_hbm), (gval, gv_hbm))):
        back = jnp.concatenate([rcv_l[i], rcv_r[i]], axis=0)
        total = acc_mid[i, RAD * CW : (RAD + CH) * CW] + dot(home, back, NN)
        gap = jnp.zeros((CELLS - RAD * CW, D), F32)
        above = up_in[i].astype(F32).reshape(RAD * CW, D)
        below = down_in[i].astype(F32).reshape(RAD * CW, D)
        total = total + jnp.concatenate([above, gap], axis=0) + jnp.concatenate([gap, below], axis=0)
        ref[...] = total.astype(BF)
        grad_stores.append(local(ref, hbm, 10 + i))
        grad_stores[-1].start()

    @pl.loop(1, NZ)
    def _(k):
        bz_copy(k).wait()

    bias_zin[0] = bias_b[1]
    bias_c[me_group] = jnp.sum(bias_zin[...], axis=0)
    bias_mine = bias_c.at[me_group]

    def bd_copy(k):
        return remote(bias_mine, bias_mine, bd_ss.at[k], bd_rs.at[k], member(k)[2])

    @pl.loop(1, GROUP)
    def _(k):
        bd_copy(k).start()

    @pl.loop(1, NY)
    def _(k):
        a3_copy(k).wait()
        ca_copy(k).start()
        b3_copy(k).wait()
        cb_copy(k).start()

    def stores(of_core, first):
        made = []
        for i in range(2):
            for j in range(2):
                lanes = pl.ds(pl.multiple_of(of_core * OUTS + i * half + j * 128, 128), 128)
                made.append(local(out.at[of_core, i, :, :, j], ow_hbm.at[:, :, :, lanes], first + 2 * i + j))
        return made

    kept = stores(core, 12)
    for c in kept:
        c.start()

    @pl.loop(1, GROUP)
    def _(k):
        bd_copy(k).wait()

    ob_ref[...] = jnp.concatenate([bias_c[i, :per, : KS * KS] for i in range(GROUP)], axis=0)

    @pl.loop(0, NY)
    def _(k):
        ca_copy(k).wait()
        cb_copy(k).wait()

    given = stores(1 - core, 16)
    for c in given:
        c.start()
    for c in (gq_store, *grad_stores, *kept, *given):
        c.wait()


def hand_over(*refs):
    sources, targets, held, sems = refs[:5], refs[5:10], refs[10:15], refs[15]
    pairs = []
    for i in range(5):
        chunks = range(NY) if i == 3 else (None,)
        for c in chunks:
            src, via, dst = (r if c is None else r.at[c] for r in (sources[i], held[i], targets[i]))
            at_sem = len(pairs)
            pairs.append(
                (pltpu.make_async_copy(src, via, sems.at[0, at_sem]), pltpu.make_async_copy(via, dst, sems.at[1, at_sem]))
            )
    for fetch, _ in pairs:
        fetch.start()
    for fetch, store in pairs:
        fetch.wait()
        store.start()
    for _, store in pairs:
        store.wait()


def on_device(queries, keys, values, grad_out, out_weight, rel_bias):
    one_hot, places, pack, spread, join, home, heads = tables()
    cells_out = jax.ShapeDtypeStruct((CELLS, D), BF)
    dma = pltpu.SemaphoreType.DMA
    vm = pltpu.VMEM
    in_hbm = pl.BlockSpec(memory_space=pl.ANY)
    in_vmem = pl.BlockSpec(memory_space=pltpu.VMEM)
    scratch = [
        vm((CH, CW, D), BF),
        vm((CH, CW, D), BF),
        vm((D, D), BF),
        vm((BQ, KEYS, 128), BF),
        vm((2, EXT, CW, D), BF),
        vm((2, 80, D), BF),
        vm((2, 80, D), BF),
        vm((2, STAGE, D), BF),
        vm((2, STAGE, D), BF),
        vm((CELLS, D), BF),
        vm((BLOCKS, KEYS, D), BF),
        vm((BLOCKS, KEYS, D), BF),
        vm((HEADS, BQ, KEYS), F32),
        vm((16, 4 * BQ, KEYS), F32),
        vm((CELLS, D), BF),
        vm((GROUP, CELLS, FEATS), BF),
        vm((GROUP, CH, CW, OUTS), BF),
        vm((HEADS, BQ, KEYS), F32),
        vm((2, EXT * CW, D), F32),
        vm((2, BLOCKS * 2 * SIDEK, D), BF),
        vm((2, STAGE, D), BF),
        vm((2, STAGE, D), BF),
        vm((2, STAGE, D), BF),
        vm((2, STAGE, D), BF),
        vm((2, RAD, CW, D), BF),
        vm((2, RAD, CW, D), BF),
        vm((2, RAD, CW, D), BF),
        vm((2, RAD, CW, D), BF),
        vm((CELLS, D), BF),
        vm((CELLS, D), BF),
        vm((CELLS, D), BF),
        vm((FEATS // PROWS, PROWS, OUTS), BF),
        vm((NX, XPIECES, PROWS, OUTS), BF),
        vm((NZ, PROWS, 256), BF),
        vm((NZ, PROWS, 256), BF),
        vm((CORES, 2, NY, NX * XPIECES, 2, PROWS, 128), BF),
        vm((GROUP, 8, 128), F32),
        vm((GROUP, 8, 128), F32),
        vm((NX, 8, 128), F32),
        vm((2, 8, 128), F32),
        vm((NZ, 8, 128), F32),
        vm((GROUP, 8, 128), F32),
        dma((20,)),
    ]
    for count in (8, GROUP, (2, GROUP), 8, NX, NZ, NZ, NX, NY, NY, NX, NY, NX, GROUP, NX, NZ, GROUP):
        shape = count if isinstance(count, tuple) else (count,)
        scratch += [dma(shape), dma(shape)]
    results = pl.pallas_call(
        kernel,
        out_shape=(
            cells_out,
            cells_out,
            cells_out,
            jax.ShapeDtypeStruct((NY, FEATS // PROWS, PROWS, D), BF),
            jax.ShapeDtypeStruct((HEADS, KS * KS), F32),
        ),
        in_specs=[in_hbm] * 5 + [in_vmem, in_hbm] + [in_vmem] * 6,
        out_specs=(in_hbm, in_hbm, in_hbm, in_hbm, in_vmem),
        scratch_shapes=scratch,
        compiler_params=pltpu.CompilerParams(
            collective_id=0, has_side_effects=True, vmem_limit_bytes=56 * 2**20
        ),
        cost_estimate=pl.CostEstimate(flops=3 * 10**9, bytes_accessed=8 * 2**20, transcendentals=10**6),
        name="attention_backward",
    )(queries, keys, values, grad_out, out_weight, rel_bias, one_hot, places, pack, spread, join, home, heads)
    gq, gk, gv, gw, gb = pl.pallas_call(
        hand_over,
        out_shape=tuple(jax.ShapeDtypeStruct(r.shape, r.dtype) for r in results),
        in_specs=[in_hbm] * 5,
        out_specs=(in_hbm,) * 5,
        scratch_shapes=[vm(r.shape, r.dtype) for r in results] + [dma((2, 4 + NY))],
        name="hand_over",
    )(*results)
    shape = queries.shape
    return gq.reshape(shape), gk.reshape(shape), gv.reshape(shape), gw.reshape(D, D), gb


def solution(mesh):
    cells = P("row", "col", None)
    return jax.shard_map(
        on_device,
        mesh=mesh,
        in_specs=(cells, cells, cells, cells, P(), P()),
        out_specs=(cells, cells, cells, P(), P()),
        check_vma=False,
    )
```

```python
import functools
import math

import jax
import jax.numpy as jnp
import numpy as np
from jax import lax
from jax.experimental import pallas as pl
from jax.experimental.pallas import tpu as pltpu
from jax.sharding import PartitionSpec as P

MESH = pl.DeviceIdType.MESH
BF = jnp.bfloat16
F32 = jnp.float32

RAD = 5
KS = 11
D = 1024
HEADS = 16
CH = 16
CW = 8
CELLS = CH * CW
XLO, NY, NZ, XHI, CORES = 2, 4, 8, 2, 2
NX = XLO * XHI
GROUP = NY * CORES
BLOCKS = 4
BROWS = CH // BLOCKS
BQ = BROWS * CW
MIDK = (BROWS + 2 * RAD) * CW
SIDEK = 72
KEYS = MIDK + 2 * SIDEK
STAGE = 144
EXT = CH + 2 * RAD
FEATS = D // NY
OUTS = D // CORES
PROWS = 16
XPIECES = FEATS // PROWS // NX
NEG = -1e30
NEIGHBOURS = ((0, -1), (0, 1), (-1, 0), (1, 0), (-1, -1), (1, -1), (-1, 1), (1, 1))


def key_places():
    rows = np.full(KEYS, 1000, np.int64)
    cols = np.full(KEYS, 1000, np.int64)
    mid = np.arange(MIDK)
    rows[:MIDK], cols[:MIDK] = mid // CW, mid % CW
    side = np.arange(70)
    for first, base in ((MIDK, -RAD), (MIDK + SIDEK, CW)):
        rows[first + 1 : first + 71] = side // RAD
        cols[first + 1 : first + 71] = base + side % RAD
    return rows, cols


def tables():
    rows, cols = key_places()
    query = np.arange(BQ)
    dr = rows[None, :] - RAD - (query // CW)[:, None]
    dc = cols[None, :] - (query % CW)[:, None]
    inside = (np.abs(dr) <= RAD) & (np.abs(dc) <= RAD)
    offsets = np.where(inside, (dr + RAD) * KS + dc + RAD, 127)
    one_hot = offsets[:, :, None] == np.arange(128)[None, None, :]
    places = np.zeros((8, KEYS), np.int32)
    places[0], places[1] = rows, cols
    pack = np.zeros((2 * 80, CELLS), bool)
    edge = np.arange(80)
    pack[edge, edge // RAD * CW + edge % RAD] = True
    pack[80 + edge, edge // RAD * CW + CW - RAD + edge % RAD] = True
    spread = np.zeros((BLOCKS * SIDEK, STAGE), bool)
    place = np.arange(70)
    for b in range(BLOCKS):
        ext = 20 * b + place
        at = np.where(ext < 25, 80 + ext, np.where(ext < 105, ext - 25, ext))
        spread[b * SIDEK + 1 + place, at] = True
    strip = np.zeros((2 * 64, 2 * RAD * CW), bool)
    corner = np.arange(50)
    strip[corner, corner // RAD * CW + corner % RAD] = True
    strip[64 + corner, corner // RAD * CW + CW - RAD + corner % RAD] = True
    join = np.zeros((2 * STAGE, BLOCKS * 2 * SIDEK), bool)
    for b in range(BLOCKS):
        place = np.arange(SIDEK)
        join[6 + 20 * b + place, 2 * SIDEK * b + place] = True
        join[STAGE + 6 + 20 * b + place, 2 * SIDEK * b + SIDEK + place] = True
    entry = np.arange(STAGE)
    cell = np.where(entry < 32, entry, np.where(entry < 112, entry - 32, entry - 64))
    home = np.zeros((CELLS, 2 * STAGE), bool)
    home[cell // RAD * CW + cell % RAD, entry] = True
    home[cell // RAD * CW + CW - RAD + cell % RAD, STAGE + entry] = True
    heads = np.repeat(np.arange(4), BQ)[:, None] == (np.arange(256) // 64)[None, :]
    as_low = lambda t: np.asarray(t, np.float32).astype(jnp.bfloat16)
    return (as_low(one_hot), places, as_low(pack), as_low(strip), as_low(spread), as_low(join), as_low(home), as_low(heads))


def dot(a, b, dims):
    return lax.dot_general(a, b, ((dims[0], dims[1]), ((), ())), preferred_element_type=F32)


NN = ((1,), (0,))
NT = ((1,), (1,))
TN = ((0,), (0,))


def kernel(
    q_hbm, k_hbm, v_hbm, g_hbm, w_hbm, bias_ref, oh_hbm, places_ref, pack_ref, strip_ref, spread_ref, join_ref, home_ref, heads_ref,
    gq, gk, gval, out, ob_ref,
    qv, gv, wv, ohv, mid, panel_l, panel_r, strip_l, strip_r, stage_l, stage_r, ga, kb, vb, table, probs, att, at, go,
    sg_sum, acc_mid, side, ret_l, ret_r, rcv_l, rcv_r, up_out, down_out, up_in, down_in,
    wt, rx, wz, rz, bias_a, bias_ain, bias_xin, bias_b, bias_zin, bias_c,
    loc_sem, halo_ss, halo_rs, go_ss, go_rs, at_ss, at_rs, ret_ss, ret_rs, rx_ss, rx_rs, rz_ss, rz_rs, zg_ss, zg_rs,
    a2_ss, a2_rs, b2_ss, b2_rs, a3_ss, a3_rs, b3_ss, b3_rs, ca_ss, ca_rs, cb_ss, cb_rs,
    ba_ss, ba_rs, bx_ss, bx_rs, bz_ss, bz_rs, bd_ss, bd_rs,
):
    row, col = lax.axis_index("row"), lax.axis_index("col")
    nrow, ncol = XLO * NY, NZ * XHI * CORES
    x = (col // CORES) % XHI * XLO + row // NY
    y, z, core = row % NY, col // (XHI * CORES), col % CORES
    scale = 1.0 / math.sqrt(D // HEADS)

    def device(x_at, y_at, z_at, core_at):
        return (x_at % XLO * NY + y_at, (z_at * XHI + x_at // XLO) * CORES + core_at)

    def neighbour(dr, dc):
        return ((row + dr + nrow) % nrow, (col + dc + ncol) % ncol)

    def member(k):
        yy = (y + k // CORES) % NY
        cc = (core + k % CORES) % CORES
        return yy, cc, device(x, yy, z, cc)

    def along_x(k):
        return device((x + k) % NX, y, z, core)

    def along_y(k):
        return device(x, (y + k) % NY, z, core)

    def along_z(k):
        return device(x, y, (z + k) % NZ, core)

    me_group = y * CORES + core

    def local(src, dst, at_sem):
        return pltpu.make_async_copy(src, dst, loc_sem.at[at_sem])

    def remote(src, dst, ss, rsem, to):
        return pltpu.make_async_remote_copy(
            src_ref=src, dst_ref=dst, send_sem=ss, recv_sem=rsem, device_id=to, device_id_type=MESH
        )

    loads = [
        local(k_hbm, mid.at[0, RAD : RAD + CH], 0),
        local(v_hbm, mid.at[1, RAD : RAD + CH], 1),
        local(g_hbm, gv, 2),
        local(w_hbm, wv, 3),
        local(q_hbm, qv, 4),
        local(oh_hbm, ohv, 5),
    ]
    for c in loads:
        c.start()
    barrier = pltpu.get_barrier_semaphore()
    for dr, dc in NEIGHBOURS:
        pl.semaphore_signal(barrier, inc=1, device_id=neighbour(dr, dc), device_id_type=MESH)

    @pl.loop(1, GROUP)
    def _(k):
        pl.semaphore_signal(barrier, inc=1, device_id=member(k)[2], device_id_type=MESH)

    @pl.loop(1, NX)
    def _(k):
        pl.semaphore_signal(barrier, inc=1, device_id=along_x(k), device_id_type=MESH)

    @pl.loop(1, NZ)
    def _(k):
        pl.semaphore_signal(barrier, inc=1, device_id=along_z(k), device_id_type=MESH)

    loads[0].wait()
    loads[1].wait()
    for i in range(2):
        own = mid[i, RAD : RAD + CH].reshape(CELLS, D)
        packed = dot(pack_ref[...], own, NN).astype(BF)
        panel_l[i] = packed[:80]
        panel_r[i] = packed[80:]
    pl.semaphore_wait(barrier, len(NEIGHBOURS) + GROUP - 1 + NX - 1 + NZ - 1)

    halo_parts = (
        (mid.at[:, RAD : 2 * RAD], mid.at[:, RAD + CH :], 2),
        (mid.at[:, CH : CH + RAD], mid.at[:, :RAD], 3),
        (panel_l, stage_r.at[:, :80], 0),
        (panel_r, stage_l.at[:, :80], 1),
        (strip_l, stage_r.at[:, 80:], 0),
        (strip_r, stage_l.at[:, 80:], 1),
    )
    halo = [
        remote(src, dst, halo_ss.at[i], halo_rs.at[i], neighbour(*NEIGHBOURS[n]))
        for i, (src, dst, n) in enumerate(halo_parts)
    ]
    for c in halo[:4]:
        c.start()

    loads[2].wait()

    def go_copy(k):
        yy, cc, to = member(k)
        lanes = pl.ds(pl.multiple_of(cc * OUTS, OUTS), OUTS)
        return remote(gv.at[:, :, lanes], go.at[me_group], go_ss.at[k], go_rs.at[k], to)

    @pl.loop(1, GROUP)
    def _(k):
        go_copy(k).start()

    own_lanes = pl.ds(pl.multiple_of(core * OUTS, OUTS), OUTS)
    go_own = local(gv.at[:, :, own_lanes], go.at[me_group], 6)
    go_own.start()

    loads[3].wait()
    ga[...] = dot(gv[...].reshape(CELLS, D), wv[...], NT).astype(BF)

    halo[0].wait()
    halo[1].wait()
    for i in range(2):
        rims = jnp.concatenate([mid[i, :RAD], mid[i, RAD + CH :]], axis=0).reshape(2 * RAD * CW, D)
        packed = dot(strip_ref[...], rims, NN).astype(BF)
        strip_l[i] = packed[:64]
        strip_r[i] = packed[64:]
    halo[4].start()
    halo[5].start()

    loads[5].wait()
    padded = jnp.concatenate([bias_ref[...], jnp.full((HEADS, 128 - KS * KS), NEG, F32)], axis=1)
    high = padded.astype(BF)
    rest = padded - high.astype(F32)
    middle = rest.astype(BF)
    low = (rest - middle.astype(F32)).astype(BF)
    three = jnp.concatenate([high, middle, low], axis=0)
    for i in range(BQ):
        terms = dot(three, ohv[i], NT)
        table[:, i, :] = terms[:HEADS] + terms[HEADS : 2 * HEADS] + terms[2 * HEADS :]
    for ref in (acc_mid, sg_sum):
        ref[...] = jnp.zeros_like(ref)

    for i, slab in enumerate((kb, vb)):
        for b in range(BLOCKS):
            slab[b, :MIDK] = mid[i, b * BROWS : b * BROWS + BROWS + 2 * RAD].reshape(MIDK, D)
    loads[4].wait()
    for c in halo[2:]:
        c.wait()
    for i, slab in enumerate((kb, vb)):
        left = dot(spread_ref[...], stage_l[i], NN)
        right = dot(spread_ref[...], stage_r[i], NN)
        for b in range(BLOCKS):
            rows = slice(b * SIDEK, (b + 1) * SIDEK)
            slab[b, MIDK:] = jnp.concatenate([left[rows], right[rows]], axis=0).astype(BF)

    mask_low = heads_ref[...]
    mask_wide = mask_low.astype(F32)

    def spread_heads(tile):
        return jnp.concatenate([tile] * 4, axis=0) * mask_low

    def fold_heads(full):
        return jnp.sum((full * mask_wide).reshape(4, BQ, 256), axis=0)

    key_row, key_col = places_ref[0:1, :], places_ref[1:2, :]
    grid_col = col * CW + key_col
    col_ok = (grid_col >= 0) & (grid_col < ncol * CW)
    q2 = qv[...].reshape(CELLS, D)
    groups = [slice(h * 256, (h + 1) * 256) for h in range(4)]

    def forward(b):
        cells = slice(b * BQ, (b + 1) * BQ)
        grid_row = row * CH + b * BROWS - RAD + key_row
        present = col_ok & (grid_row >= 0) & (grid_row < nrow * CH)
        absent = jnp.where(present, 0.0, NEG)
        scores = [dot(spread_heads(q2[cells, n]), kb[b, :, n], NT) for n in groups]
        scores = [
            s * scale + (table[4 * h : 4 * h + 4].reshape(4 * BQ, KEYS) + absent) for h, s in enumerate(scores)
        ]
        weights = [jnp.exp(s - jnp.max(s, axis=1, keepdims=True)) for s in scores]
        p = [e * (1.0 / jnp.sum(e, axis=1, keepdims=True)) for e in weights]
        for h in range(4):
            probs[b * 4 + h] = p[h]
        full = [dot(t.astype(BF), vb[b, :, n], NN) for t, n in zip(p, groups)]
        for t, n in zip(full, groups):
            att[cells, n] = fold_heads(t).astype(BF)

    half_cells = CELLS // 2

    def at_copy(part, k):
        yy, cc, to = member(k)
        src = att.at[pl.ds(part * half_cells, half_cells), pl.ds(pl.multiple_of(yy * FEATS, FEATS), FEATS)]
        dst = at.at[me_group, pl.ds(part * half_cells, half_cells)]
        return remote(src, dst, at_ss.at[part, k], at_rs.at[part, k], to)

    for part in range(2):
        forward(2 * part)
        forward(2 * part + 1)

        @pl.loop(1, GROUP)
        def _(k):
            at_copy(part, k).start()

    at_own = local(att.at[:, pl.ds(pl.multiple_of(y * FEATS, FEATS), FEATS)], at.at[me_group], 7)
    at_own.start()

    def backward(b):
        cells = slice(b * BQ, (b + 1) * BQ)
        qm = [spread_heads(q2[cells, n]) for n in groups]
        gm = [spread_heads(ga[cells, n]) for n in groups]
        p = [probs[b * 4 + h] for h in range(4)]
        dp = [dot(g, vb[b, :, n], NT) for g, n in zip(gm, groups)]
        sg = [t * (d - jnp.sum(t * d, axis=1, keepdims=True)) for t, d in zip(p, dp)]
        for h in range(4):
            sg_sum[4 * h : 4 * h + 4] += sg[h].reshape(4, BQ, KEYS)
        sl = [t.astype(BF) for t in sg]
        for h, n in enumerate(groups):
            gq[cells, n] = (fold_heads(dot(sl[h], kb[b, :, n], NN)) * scale).astype(BF)
            parts = (dot(sl[h], qm[h], TN) * scale, dot(p[h].astype(BF), gm[h], TN))
            for i, part in enumerate(parts):
                acc_mid[i, b * BQ : b * BQ + MIDK, n] += part[:MIDK]
                side[i, b * 2 * SIDEK : (b + 1) * 2 * SIDEK, n] = part[MIDK:].astype(BF)

    backward(0)
    backward(1)
    go_own.wait()
    at_own.wait()

    @pl.loop(1, GROUP)
    def _(k):
        go_copy(k).wait()
        at_copy(0, k).wait()
        at_copy(1, k).wait()

    wt[...] = dot(at[...].reshape(GROUP * CELLS, FEATS), go[...].reshape(GROUP * CELLS, OUTS), TN).reshape(FEATS // PROWS, PROWS, OUTS).astype(BF)

    def rx_copy(k):
        part = wt.at[pl.ds((x + k) % NX * XPIECES, XPIECES)]
        return remote(part, rx.at[k], rx_ss.at[k], rx_rs.at[k], along_x(k))

    @pl.loop(1, NX)
    def _(k):
        rx_copy(k).start()

    rx_own = local(wt.at[pl.ds(x * XPIECES, XPIECES)], rx.at[0], 8)
    rx_own.start()
    backward(2)
    backward(3)

    for i in range(2):
        joined = dot(join_ref[...], side[i], NN).astype(BF)
        ret_l[i] = joined[:STAGE]
        ret_r[i] = joined[STAGE:]
    up_out[...] = acc_mid[:, : RAD * CW].reshape(2, RAD, CW, D).astype(BF)
    down_out[...] = acc_mid[:, (RAD + CH) * CW :].reshape(2, RAD, CW, D).astype(BF)
    ret_parts = (
        (ret_l.at[:, 32:112], rcv_r.at[:, 32:112]),
        (ret_r.at[:, 32:112], rcv_l.at[:, 32:112]),
        (up_out, down_in),
        (down_out, up_in),
        (ret_l.at[:, 0:32], rcv_r.at[:, 112:144]),
        (ret_l.at[:, 112:144], rcv_r.at[:, 0:32]),
        (ret_r.at[:, 0:32], rcv_l.at[:, 112:144]),
        (ret_r.at[:, 112:144], rcv_l.at[:, 0:32]),
    )
    ret = [
        remote(src, dst, ret_ss.at[i], ret_rs.at[i], neighbour(*NEIGHBOURS[i]))
        for i, (src, dst) in enumerate(ret_parts)
    ]

    rx_own.wait()

    @pl.loop(1, NX)
    def _(k):
        rx_copy(k).wait()

    total = jnp.sum(rx[...].astype(F32), axis=0).astype(BF)
    half = OUTS // 2
    for i in range(XPIECES):
        for j in range(2):
            first, second = total[i, :, j * 128 : j * 128 + 128], total[i, :, half + j * 128 : half + j * 128 + 128]
            wz[2 * i + j] = jnp.concatenate([first, second], axis=1)

    def rz_copy(k):
        return remote(wz.at[(z + k) % NZ], rz.at[k], rz_ss.at[k], rz_rs.at[k], along_z(k))

    @pl.loop(1, NZ)
    def _(k):
        rz_copy(k).start()

    for c in ret:
        c.start()

    bias_sum = jnp.zeros((2 * HEADS, 128), F32)
    for i in range(BQ):
        sums = sg_sum[:, i, :]
        high = sums.astype(BF)
        low = (sums - high.astype(F32)).astype(BF)
        bias_sum = bias_sum + dot(jnp.concatenate([high, low], axis=0), ohv[i], NN)
    bias_sum = bias_sum[:HEADS] + bias_sum[HEADS:]
    per = HEADS // GROUP
    bias_a[...] = jnp.zeros_like(bias_a)
    for i in range(GROUP):
        bias_a[i, :per] = bias_sum[i * per : (i + 1) * per]

    def ba_copy(k):
        yy, cc, to = member(k)
        return remote(bias_a.at[yy * CORES + cc], bias_ain.at[k], ba_ss.at[k], ba_rs.at[k], to)

    @pl.loop(1, GROUP)
    def _(k):
        ba_copy(k).start()

    rz[0] = wz[z]

    @pl.loop(1, NZ)
    def _(k):
        rz_copy(k).wait()

    final = jnp.sum(rz[...].astype(F32), axis=0).astype(BF)
    spot = x * XPIECES + z // 2
    out[core, 0, y, spot, z % 2] = final[:, :128]
    out[core, 1, y, spot, z % 2] = final[:, 128:]
    mine = out.at[core, :, y, spot, z % 2]

    def zg_copy(k):
        return remote(mine, mine, zg_ss.at[k], zg_rs.at[k], along_z(k))

    @pl.loop(1, NZ)
    def _(k):
        zg_copy(k).start()

    @pl.loop(1, GROUP)
    def _(k):
        ba_copy(k).wait()

    bias_ain[0] = bias_a[me_group]
    bias_b[0] = jnp.sum(bias_ain[...], axis=0)

    def bx_copy(k):
        return remote(bias_b.at[0], bias_xin.at[k], bx_ss.at[k], bx_rs.at[k], along_x(k))

    def bz_copy(k):
        return remote(bias_b.at[1], bias_zin.at[k], bz_ss.at[k], bz_rs.at[k], along_z(k))

    @pl.loop(1, NX)
    def _(k):
        bx_copy(k).start()

    @pl.loop(1, NZ)
    def _(k):
        zg_copy(k).wait()

    slab_a = out.at[core, 0, y, pl.ds(x * XPIECES, XPIECES)]
    slab_b = out.at[core, 1, y, pl.ds(x * XPIECES, XPIECES)]

    def a2_copy(k):
        return remote(slab_a, slab_a, a2_ss.at[k], a2_rs.at[k], along_x(k))

    def b2_copy(k):
        return remote(slab_b, slab_b, b2_ss.at[k], b2_rs.at[k], along_y(k))

    @pl.loop(1, NX)
    def _(k):
        a2_copy(k).start()

    @pl.loop(1, NY)
    def _(k):
        b2_copy(k).start()

    @pl.loop(1, NX)
    def _(k):
        bx_copy(k).wait()

    bias_xin[0] = bias_b[0]
    bias_b[1] = jnp.sum(bias_xin[...], axis=0)

    @pl.loop(1, NZ)
    def _(k):
        bz_copy(k).start()

    def part_a(k):
        return out.at[core, 0, (y + k + NY) % NY]

    def part_b(k):
        return out.at[core, 1, :, pl.ds((x + k + NX) % NX * XPIECES, XPIECES)]

    def a3_copy(k):
        return remote(part_a(0), part_a(0), a3_ss.at[k], a3_rs.at[k], along_y(k))

    def b3_copy(k):
        return remote(part_b(0), part_b(0), b3_ss.at[k], b3_rs.at[k], along_x(k))

    def ca_copy(k):
        return remote(part_a(-k), part_a(-k), ca_ss.at[k], ca_rs.at[k], device(x, y, z, 1 - core))

    def cb_copy(k):
        return remote(part_b(-k), part_b(-k), cb_ss.at[k], cb_rs.at[k], device(x, y, z, 1 - core))

    @pl.loop(1, NX)
    def _(k):
        a2_copy(k).wait()

    @pl.loop(1, NY)
    def _(k):
        a3_copy(k).start()

    @pl.loop(1, NY)
    def _(k):
        b2_copy(k).wait()

    @pl.loop(1, NX)
    def _(k):
        b3_copy(k).start()

    ca_copy(0).start()
    cb_copy(0).start()

    for c in ret:
        c.wait()
    home = home_ref[...]
    for i, ref in enumerate((gk, gval)):
        back = jnp.concatenate([rcv_l[i], rcv_r[i]], axis=0)
        total = acc_mid[i, RAD * CW : (RAD + CH) * CW] + dot(home, back, NN)
        gap = jnp.zeros((CELLS - RAD * CW, D), F32)
        above = up_in[i].astype(F32).reshape(RAD * CW, D)
        below = down_in[i].astype(F32).reshape(RAD * CW, D)
        total = total + jnp.concatenate([above, gap], axis=0) + jnp.concatenate([gap, below], axis=0)
        ref[...] = total.astype(BF)

    @pl.loop(1, NZ)
    def _(k):
        bz_copy(k).wait()

    bias_zin[0] = bias_b[1]
    bias_c[me_group] = jnp.sum(bias_zin[...], axis=0)
    bias_mine = bias_c.at[me_group]

    def bd_copy(k):
        return remote(bias_mine, bias_mine, bd_ss.at[k], bd_rs.at[k], member(k)[2])

    @pl.loop(1, GROUP)
    def _(k):
        bd_copy(k).start()

    @pl.loop(1, NY)
    def _(k):
        a3_copy(k).wait()
        ca_copy(k).start()
        b3_copy(k).wait()
        cb_copy(k).start()

    @pl.loop(1, GROUP)
    def _(k):
        bd_copy(k).wait()

    ob_ref[...] = jnp.concatenate([bias_c[i, :per, : KS * KS] for i in range(GROUP)], axis=0)

    @pl.loop(0, NY)
    def _(k):
        ca_copy(k).wait()
        cb_copy(k).wait()


def hand_over(*refs):
    sources, targets, sems = refs[:5], refs[5:10], refs[10]
    pairs = [(sources[i], targets[i]) for i in (0, 1, 2, 4)]
    for c in range(CORES):
        for i in range(2):
            for j in range(2):
                first = c * OUTS + i * OUTS // 2 + j * 128
                pairs.append((sources[3].at[c, i, :, :, j], targets[3].at[:, :, :, first : first + 128]))
    copies = [pltpu.make_async_copy(src, dst, sems.at[i]) for i, (src, dst) in enumerate(pairs)]
    for c in copies:
        c.start()
    for c in copies:
        c.wait()


def on_device(queries, keys, values, grad_out, out_weight, rel_bias):
    one_hot, places, pack, strip, spread, join, home, heads = tables()
    cells_out = jax.ShapeDtypeStruct((CELLS, D), BF)
    dma = pltpu.SemaphoreType.DMA
    vm = pltpu.VMEM
    in_hbm = pl.BlockSpec(memory_space=pltpu.HBM)
    in_vmem = pl.BlockSpec(memory_space=pltpu.VMEM)
    scratch = [
        vm((CH, CW, D), BF),
        vm((CH, CW, D), BF),
        vm((D, D), BF),
        vm((BQ, KEYS, 128), BF),
        vm((2, EXT, CW, D), BF),
        vm((2, 80, D), BF),
        vm((2, 80, D), BF),
        vm((2, 64, D), BF),
        vm((2, 64, D), BF),
        vm((2, STAGE, D), BF),
        vm((2, STAGE, D), BF),
        vm((CELLS, D), BF),
        vm((BLOCKS, KEYS, D), BF),
        vm((BLOCKS, KEYS, D), BF),
        vm((HEADS, BQ, KEYS), F32),
        vm((16, 4 * BQ, KEYS), F32),
        vm((CELLS, D), BF),
        vm((GROUP, CELLS, FEATS), BF),
        vm((GROUP, CH, CW, OUTS), BF),
        vm((HEADS, BQ, KEYS), F32),
        vm((2, EXT * CW, D), F32),
        vm((2, BLOCKS * 2 * SIDEK, D), BF),
        vm((2, STAGE, D), BF),
        vm((2, STAGE, D), BF),
        vm((2, STAGE, D), BF),
        vm((2, STAGE, D), BF),
        vm((2, RAD, CW, D), BF),
        vm((2, RAD, CW, D), BF),
        vm((2, RAD, CW, D), BF),
        vm((2, RAD, CW, D), BF),
        vm((FEATS // PROWS, PROWS, OUTS), BF),
        vm((NX, XPIECES, PROWS, OUTS), BF),
        vm((NZ, PROWS, 256), BF),
        vm((NZ, PROWS, 256), BF),
        vm((GROUP, 8, 128), F32),
        vm((GROUP, 8, 128), F32),
        vm((NX, 8, 128), F32),
        vm((2, 8, 128), F32),
        vm((NZ, 8, 128), F32),
        vm((GROUP, 8, 128), F32),
        dma((9,)),
    ]
    for count in (8, GROUP, (2, GROUP), 8, NX, NZ, NZ, NX, NY, NY, NX, NY, NX, GROUP, NX, NZ, GROUP):
        shape = count if isinstance(count, tuple) else (count,)
        scratch += [dma(shape), dma(shape)]
    results = pl.pallas_call(
        kernel,
        out_shape=(
            vm((CELLS, D), BF),
            vm((CELLS, D), BF),
            vm((CELLS, D), BF),
            vm((CORES, 2, NY, NX * XPIECES, 2, PROWS, 128), BF),
            vm((HEADS, KS * KS), F32),
        ),
        in_specs=[in_hbm] * 5 + [in_vmem, in_hbm] + [in_vmem] * 7,
        out_specs=(in_vmem,) * 5,
        scratch_shapes=scratch,
        compiler_params=pltpu.CompilerParams(
            collective_id=0, has_side_effects=True, vmem_limit_bytes=56 * 2**20
        ),
        cost_estimate=pl.CostEstimate(flops=3 * 10**9, bytes_accessed=8 * 2**20, transcendentals=10**6),
        name="attention_backward",
    )(queries, keys, values, grad_out, out_weight, rel_bias, one_hot, places, pack, strip, spread, join, home, heads)
    gq, gk, gv, gw, gb = pl.pallas_call(
        hand_over,
        out_shape=(
            cells_out,
            cells_out,
            cells_out,
            jax.ShapeDtypeStruct((NY, FEATS // PROWS, PROWS, D), BF),
            jax.ShapeDtypeStruct((HEADS, KS * KS), F32),
        ),
        in_specs=[in_vmem] * 5,
        out_specs=(in_hbm,) * 5,
        scratch_shapes=[dma((4 + 4 * CORES,))],
        name="hand_over",
    )(*(pltpu.with_memory_space_constraint(r, pltpu.VMEM) for r in results))
    shape = queries.shape
    return gq.reshape(shape), gk.reshape(shape), gv.reshape(shape), gw.reshape(D, D), gb


def solution(mesh):
    cells = P("row", "col", None)
    return jax.shard_map(
        on_device,
        mesh=mesh,
        in_specs=(cells, cells, cells, cells, P(), P()),
        out_specs=(cells, cells, cells, P(), P()),
        check_vma=False,
    )
```

```python
import functools
import math

import jax
import jax.numpy as jnp
import numpy as np
from jax import lax
from jax.experimental import pallas as pl
from jax.experimental.pallas import tpu as pltpu
from jax.sharding import PartitionSpec as P

MESH = pl.DeviceIdType.MESH
BF = jnp.bfloat16
F32 = jnp.float32

RAD = 5
KS = 11
D = 1024
HEADS = 16
CH = 16
CW = 8
CELLS = CH * CW
XLO, NY, NZ, XHI, CORES = 2, 4, 8, 2, 2
NX = XLO * XHI
GROUP = NY * CORES
BLOCKS = 4
BROWS = CH // BLOCKS
BQ = BROWS * CW
MIDK = (BROWS + 2 * RAD) * CW
SIDEK = 72
KEYS = MIDK + 2 * SIDEK
STAGE = 144
EXT = CH + 2 * RAD
FEATS = D // NY
OUTS = D // CORES
PROWS = 16
XPIECES = FEATS // PROWS // NX
NEG = -1e30
NEIGHBOURS = ((0, -1), (0, 1), (-1, 0), (1, 0))


def key_places():
    rows = np.full(KEYS, 1000, np.int64)
    cols = np.full(KEYS, 1000, np.int64)
    mid = np.arange(MIDK)
    rows[:MIDK], cols[:MIDK] = mid // CW, mid % CW
    side = np.arange(70)
    for first, base in ((MIDK, -RAD), (MIDK + SIDEK, CW)):
        rows[first + 1 : first + 71] = side // RAD
        cols[first + 1 : first + 71] = base + side % RAD
    return rows, cols


def tables():
    rows, cols = key_places()
    query = np.arange(BQ)
    dr = rows[None, :] - RAD - (query // CW)[:, None]
    dc = cols[None, :] - (query % CW)[:, None]
    inside = (np.abs(dr) <= RAD) & (np.abs(dc) <= RAD)
    offsets = np.where(inside, (dr + RAD) * KS + dc + RAD, 127)
    one_hot = offsets[:, :, None] == np.arange(128)[None, None, :]
    places = np.zeros((8, KEYS), np.int32)
    places[0], places[1] = rows, cols
    pack = np.zeros((2 * 80, CELLS), bool)
    edge = np.arange(80)
    pack[edge, edge // RAD * CW + edge % RAD] = True
    pack[80 + edge, edge // RAD * CW + CW - RAD + edge % RAD] = True
    spread = np.zeros((BLOCKS * SIDEK, STAGE), bool)
    place = np.arange(70)
    for b in range(BLOCKS):
        ext = 20 * b + place
        at = np.where(ext < 25, 80 + ext, np.where(ext < 105, ext - 25, ext))
        spread[b * SIDEK + 1 + place, at] = True
    strip = np.zeros((2 * 64, 2 * RAD * CW), bool)
    corner = np.arange(50)
    strip[corner, corner // RAD * CW + corner % RAD] = True
    strip[64 + corner, corner // RAD * CW + CW - RAD + corner % RAD] = True
    join = np.zeros((2 * STAGE, BLOCKS * 2 * SIDEK), bool)
    for b in range(BLOCKS):
        at = spread[b * SIDEK : (b + 1) * SIDEK].T
        join[:STAGE, 2 * SIDEK * b : 2 * SIDEK * b + SIDEK] = at
        join[STAGE:, 2 * SIDEK * b + SIDEK : 2 * SIDEK * (b + 1)] = at
    heads = np.repeat(np.arange(4), BQ)[:, None] == (np.arange(256) // 64)[None, :]
    as_low = lambda t: np.asarray(t, np.float32).astype(jnp.bfloat16)
    return (as_low(one_hot), places, as_low(pack), as_low(strip), as_low(spread), as_low(join), as_low(heads))


def dot(a, b, dims):
    return lax.dot_general(a, b, ((dims[0], dims[1]), ((), ())), preferred_element_type=F32)


NN = ((1,), (0,))
NT = ((1,), (1,))
TN = ((0,), (0,))


def kernel(
    q_hbm, k_hbm, v_hbm, g_hbm, w_hbm, bias_ref, oh_hbm, places_ref, pack_ref, strip_ref, spread_ref, join_ref, heads_ref,
    gq, gk, gval, out, ob_ref,
    qv, gv, wv, ohv, mid, panel_l, panel_r, strip_l, strip_r, stage_l, stage_r, ga, kb, vb, table, probs, att, at, go,
    sg_sum, acc_mid, side, ret_l, ret_r, rcv_l, rcv_r, up_out, down_out, up_in, down_in,
    wt, rx, wz, rz, bias_a, bias_ain, bias_xin, bias_b, bias_zin, bias_c,
    loc_sem, halo_ss, halo_rs, go_ss, go_rs, at_ss, at_rs, ret_ss, ret_rs, rx_ss, rx_rs, rz_ss, rz_rs, zg_ss, zg_rs,
    a2_ss, a2_rs, b2_ss, b2_rs, a3_ss, a3_rs, b3_ss, b3_rs, ca_ss, ca_rs, cb_ss, cb_rs,
    ba_ss, ba_rs, bx_ss, bx_rs, bz_ss, bz_rs, bd_ss, bd_rs,
):
    row, col = lax.axis_index("row"), lax.axis_index("col")
    nrow, ncol = XLO * NY, NZ * XHI * CORES
    x = (col // CORES) % XHI * XLO + row // NY
    y, z, core = row % NY, col // (XHI * CORES), col % CORES
    scale = 1.0 / math.sqrt(D // HEADS)

    def device(x_at, y_at, z_at, core_at):
        return (x_at % XLO * NY + y_at, (z_at * XHI + x_at // XLO) * CORES + core_at)

    def neighbour(dr, dc):
        return ((row + dr + nrow) % nrow, (col + dc + ncol) % ncol)

    def member(k):
        yy = (y + k // CORES) % NY
        cc = (core + k % CORES) % CORES
        return yy, cc, device(x, yy, z, cc)

    def along_x(k):
        return device((x + k) % NX, y, z, core)

    def along_y(k):
        return device(x, (y + k) % NY, z, core)

    def along_z(k):
        return device(x, y, (z + k) % NZ, core)

    me_group = y * CORES + core

    def local(src, dst, at_sem):
        return pltpu.make_async_copy(src, dst, loc_sem.at[at_sem])

    def remote(src, dst, ss, rsem, to):
        return pltpu.make_async_remote_copy(
            src_ref=src, dst_ref=dst, send_sem=ss, recv_sem=rsem, device_id=to, device_id_type=MESH
        )

    loads = [
        local(k_hbm, mid.at[0, RAD : RAD + CH], 0),
        local(v_hbm, mid.at[1, RAD : RAD + CH], 1),
        local(g_hbm, gv, 2),
        local(w_hbm, wv, 3),
        local(q_hbm, qv, 4),
        local(oh_hbm, ohv, 5),
    ]
    for c in loads:
        c.start()
    barrier = pltpu.get_barrier_semaphore()
    for dr, dc in NEIGHBOURS:
        pl.semaphore_signal(barrier, inc=1, device_id=neighbour(dr, dc), device_id_type=MESH)

    @pl.loop(1, GROUP)
    def _(k):
        pl.semaphore_signal(barrier, inc=1, device_id=member(k)[2], device_id_type=MESH)

    @pl.loop(1, NX)
    def _(k):
        pl.semaphore_signal(barrier, inc=1, device_id=along_x(k), device_id_type=MESH)

    @pl.loop(1, NZ)
    def _(k):
        pl.semaphore_signal(barrier, inc=1, device_id=along_z(k), device_id_type=MESH)

    loads[0].wait()
    loads[1].wait()
    for i in range(2):
        own = mid[i, RAD : RAD + CH].reshape(CELLS, D)
        packed = dot(pack_ref[...], own, NN).astype(BF)
        panel_l[i] = packed[:80]
        panel_r[i] = packed[80:]
    pl.semaphore_wait(barrier, len(NEIGHBOURS) + GROUP - 1 + NX - 1 + NZ - 1)

    halo_parts = (
        (mid.at[:, RAD : 2 * RAD], mid.at[:, RAD + CH :], 2),
        (mid.at[:, CH : CH + RAD], mid.at[:, :RAD], 3),
        (panel_l, stage_r.at[:, :80], 0),
        (panel_r, stage_l.at[:, :80], 1),
        (strip_l, stage_r.at[:, 80:], 0),
        (strip_r, stage_l.at[:, 80:], 1),
    )
    halo = [
        remote(src, dst, halo_ss.at[i], halo_rs.at[i], neighbour(*NEIGHBOURS[n]))
        for i, (src, dst, n) in enumerate(halo_parts)
    ]
    for c in halo[:4]:
        c.start()

    loads[2].wait()

    def go_copy(k):
        yy, cc, to = member(k)
        lanes = pl.ds(pl.multiple_of(cc * OUTS, OUTS), OUTS)
        return remote(gv.at[:, :, lanes], go.at[me_group], go_ss.at[k], go_rs.at[k], to)

    @pl.loop(1, GROUP)
    def _(k):
        go_copy(k).start()

    own_lanes = pl.ds(pl.multiple_of(core * OUTS, OUTS), OUTS)
    go_own = local(gv.at[:, :, own_lanes], go.at[me_group], 6)
    go_own.start()

    loads[3].wait()
    ga[...] = dot(gv[...].reshape(CELLS, D), wv[...], NT).astype(BF)

    halo[0].wait()
    halo[1].wait()
    for i in range(2):
        rims = jnp.concatenate([mid[i, :RAD], mid[i, RAD + CH :]], axis=0).reshape(2 * RAD * CW, D)
        packed = dot(strip_ref[...], rims, NN).astype(BF)
        strip_l[i] = packed[:64]
        strip_r[i] = packed[64:]
    halo[4].start()
    halo[5].start()

    loads[5].wait()
    padded = jnp.concatenate([bias_ref[...], jnp.full((HEADS, 128 - KS * KS), NEG, F32)], axis=1)
    high = padded.astype(BF)
    rest = padded - high.astype(F32)
    middle = rest.astype(BF)
    low = (rest - middle.astype(F32)).astype(BF)
    three = jnp.concatenate([high, middle, low], axis=0)
    for i in range(BQ):
        terms = dot(three, ohv[i], NT)
        table[:, i, :] = terms[:HEADS] + terms[HEADS : 2 * HEADS] + terms[2 * HEADS :]
    for ref in (acc_mid, sg_sum):
        ref[...] = jnp.zeros_like(ref)

    for i, slab in enumerate((kb, vb)):
        for b in range(BLOCKS):
            slab[b, :MIDK] = mid[i, b * BROWS : b * BROWS + BROWS + 2 * RAD].reshape(MIDK, D)
    loads[4].wait()
    for c in halo[2:]:
        c.wait()
    for i, slab in enumerate((kb, vb)):
        left = dot(spread_ref[...], stage_l[i], NN)
        right = dot(spread_ref[...], stage_r[i], NN)
        for b in range(BLOCKS):
            rows = slice(b * SIDEK, (b + 1) * SIDEK)
            slab[b, MIDK:] = jnp.concatenate([left[rows], right[rows]], axis=0).astype(BF)

    mask_low = heads_ref[...]
    mask_wide = mask_low.astype(F32)

    def spread_heads(tile):
        return jnp.concatenate([tile] * 4, axis=0) * mask_low

    def fold_heads(full):
        return jnp.sum((full * mask_wide).reshape(4, BQ, 256), axis=0)

    key_row, key_col = places_ref[0:1, :], places_ref[1:2, :]
    grid_col = col * CW + key_col
    col_ok = (grid_col >= 0) & (grid_col < ncol * CW)
    q2 = qv[...].reshape(CELLS, D)
    groups = [slice(h * 256, (h + 1) * 256) for h in range(4)]

    def forward(b):
        cells = slice(b * BQ, (b + 1) * BQ)
        grid_row = row * CH + b * BROWS - RAD + key_row
        present = col_ok & (grid_row >= 0) & (grid_row < nrow * CH)
        absent = jnp.where(present, 0.0, NEG)
        scores = [dot(spread_heads(q2[cells, n]), kb[b, :, n], NT) for n in groups]
        scores = [
            s * scale + (table[4 * h : 4 * h + 4].reshape(4 * BQ, KEYS) + absent) for h, s in enumerate(scores)
        ]
        weights = [jnp.exp(s - jnp.max(s, axis=1, keepdims=True)) for s in scores]
        p = [e * (1.0 / jnp.sum(e, axis=1, keepdims=True)) for e in weights]
        for h in range(4):
            probs[b * 4 + h] = p[h]
        full = [dot(t.astype(BF), vb[b, :, n], NN) for t, n in zip(p, groups)]
        for t, n in zip(full, groups):
            att[cells, n] = fold_heads(t).astype(BF)

    half_cells = CELLS // 2

    def at_copy(part, k):
        yy, cc, to = member(k)
        src = att.at[pl.ds(part * half_cells, half_cells), pl.ds(pl.multiple_of(yy * FEATS, FEATS), FEATS)]
        dst = at.at[me_group, pl.ds(part * half_cells, half_cells)]
        return remote(src, dst, at_ss.at[part, k], at_rs.at[part, k], to)

    for part in range(2):
        forward(2 * part)
        forward(2 * part + 1)

        @pl.loop(1, GROUP)
        def _(k):
            at_copy(part, k).start()

    at_own = local(att.at[:, pl.ds(pl.multiple_of(y * FEATS, FEATS), FEATS)], at.at[me_group], 7)
    at_own.start()

    def backward(b):
        cells = slice(b * BQ, (b + 1) * BQ)
        qm = [spread_heads(q2[cells, n]) for n in groups]
        gm = [spread_heads(ga[cells, n]) for n in groups]
        p = [probs[b * 4 + h] for h in range(4)]
        dp = [dot(g, vb[b, :, n], NT) for g, n in zip(gm, groups)]
        sg = [t * (d - jnp.sum(t * d, axis=1, keepdims=True)) for t, d in zip(p, dp)]
        for h in range(4):
            sg_sum[4 * h : 4 * h + 4] += sg[h].reshape(4, BQ, KEYS)
        sl = [t.astype(BF) for t in sg]
        for h, n in enumerate(groups):
            gq[cells, n] = (fold_heads(dot(sl[h], kb[b, :, n], NN)) * scale).astype(BF)
            parts = (dot(sl[h], qm[h], TN) * scale, dot(p[h].astype(BF), gm[h], TN))
            for i, part in enumerate(parts):
                acc_mid[i, b * BQ : b * BQ + MIDK, n] += part[:MIDK]
                side[i, b * 2 * SIDEK : (b + 1) * 2 * SIDEK, n] = part[MIDK:].astype(BF)

    backward(0)
    backward(1)
    go_own.wait()
    at_own.wait()

    @pl.loop(1, GROUP)
    def _(k):
        go_copy(k).wait()
        at_copy(0, k).wait()
        at_copy(1, k).wait()

    wt[...] = dot(at[...].reshape(GROUP * CELLS, FEATS), go[...].reshape(GROUP * CELLS, OUTS), TN).reshape(FEATS // PROWS, PROWS, OUTS).astype(BF)

    def rx_copy(k):
        part = wt.at[pl.ds((x + k) % NX * XPIECES, XPIECES)]
        return remote(part, rx.at[k], rx_ss.at[k], rx_rs.at[k], along_x(k))

    @pl.loop(1, NX)
    def _(k):
        rx_copy(k).start()

    rx_own = local(wt.at[pl.ds(x * XPIECES, XPIECES)], rx.at[0], 8)
    rx_own.start()
    backward(2)
    backward(3)

    for i in range(2):
        joined = dot(join_ref[...], side[i], NN).astype(BF)
        ret_l[i] = joined[:STAGE]
        ret_r[i] = joined[STAGE:]
    ret_parts = (
        (ret_l.at[:, 80:], rcv_r.at[:, 80:], 0),
        (ret_r.at[:, 80:], rcv_l.at[:, 80:], 1),
        (ret_l.at[:, :80], rcv_r.at[:, :80], 0),
        (ret_r.at[:, :80], rcv_l.at[:, :80], 1),
        (up_out, down_in, 2),
        (down_out, up_in, 3),
    )
    ret = [
        remote(src, dst, ret_ss.at[i], ret_rs.at[i], neighbour(*NEIGHBOURS[n]))
        for i, (src, dst, n) in enumerate(ret_parts)
    ]

    rx_own.wait()

    @pl.loop(1, NX)
    def _(k):
        rx_copy(k).wait()

    total = jnp.sum(rx[...].astype(F32), axis=0).astype(BF)
    half = OUTS // 2
    for i in range(XPIECES):
        for j in range(2):
            first, second = total[i, :, j * 128 : j * 128 + 128], total[i, :, half + j * 128 : half + j * 128 + 128]
            wz[2 * i + j] = jnp.concatenate([first, second], axis=1)

    def rz_copy(k):
        return remote(wz.at[(z + k) % NZ], rz.at[k], rz_ss.at[k], rz_rs.at[k], along_z(k))

    @pl.loop(1, NZ)
    def _(k):
        rz_copy(k).start()

    for c in ret[:4]:
        c.start()

    rz[0] = wz[z]

    @pl.loop(1, NZ)
    def _(k):
        rz_copy(k).wait()

    final = jnp.sum(rz[...].astype(F32), axis=0).astype(BF)
    spot = x * XPIECES + z // 2
    out[core, 0, y, spot, z % 2] = final[:, :128]
    out[core, 1, y, spot, z % 2] = final[:, 128:]
    mine = out.at[core, :, y, spot, z % 2]

    def zg_copy(k):
        return remote(mine, mine, zg_ss.at[k], zg_rs.at[k], along_z(k))

    @pl.loop(1, NZ)
    def _(k):
        zg_copy(k).start()

    bias_sum = jnp.zeros((2 * HEADS, 128), F32)
    for i in range(BQ):
        sums = sg_sum[:, i, :]
        high = sums.astype(BF)
        low = (sums - high.astype(F32)).astype(BF)
        bias_sum = bias_sum + dot(jnp.concatenate([high, low], axis=0), ohv[i], NN)
    bias_sum = bias_sum[:HEADS] + bias_sum[HEADS:]
    per = HEADS // GROUP
    bias_a[...] = jnp.zeros_like(bias_a)
    for i in range(GROUP):
        bias_a[i, :per] = bias_sum[i * per : (i + 1) * per]

    def ba_copy(k):
        yy, cc, to = member(k)
        return remote(bias_a.at[yy * CORES + cc], bias_ain.at[k], ba_ss.at[k], ba_rs.at[k], to)

    @pl.loop(1, GROUP)
    def _(k):
        ba_copy(k).start()

    @pl.loop(1, NZ)
    def _(k):
        zg_copy(k).wait()

    slab_a = out.at[core, 0, y, pl.ds(x * XPIECES, XPIECES)]
    slab_b = out.at[core, 1, y, pl.ds(x * XPIECES, XPIECES)]

    def a2_copy(k):
        return remote(slab_a, slab_a, a2_ss.at[k], a2_rs.at[k], along_x(k))

    def b2_copy(k):
        return remote(slab_b, slab_b, b2_ss.at[k], b2_rs.at[k], along_y(k))

    @pl.loop(1, NX)
    def _(k):
        a2_copy(k).start()

    @pl.loop(1, NY)
    def _(k):
        b2_copy(k).start()

    ret[0].wait()
    ret[1].wait()
    for i in range(2):
        back = jnp.concatenate([rcv_l[i, 80:], rcv_r[i, 80:]], axis=0)
        corners = dot(strip_ref[...], back, TN)
        rim = RAD * CW
        up_out[i] = (acc_mid[i, :rim] + corners[:rim]).reshape(RAD, CW, D).astype(BF)
        down_out[i] = (acc_mid[i, rim + CELLS :] + corners[rim:]).reshape(RAD, CW, D).astype(BF)
    ret[4].start()
    ret[5].start()

    @pl.loop(1, GROUP)
    def _(k):
        ba_copy(k).wait()

    bias_ain[0] = bias_a[me_group]
    bias_b[0] = jnp.sum(bias_ain[...], axis=0)

    def bx_copy(k):
        return remote(bias_b.at[0], bias_xin.at[k], bx_ss.at[k], bx_rs.at[k], along_x(k))

    def bz_copy(k):
        return remote(bias_b.at[1], bias_zin.at[k], bz_ss.at[k], bz_rs.at[k], along_z(k))

    @pl.loop(1, NX)
    def _(k):
        bx_copy(k).start()

    def part_a(k):
        return out.at[core, 0, (y + k + NY) % NY]

    def part_b(k):
        return out.at[core, 1, :, pl.ds((x + k + NX) % NX * XPIECES, XPIECES)]

    def a3_copy(k):
        return remote(part_a(0), part_a(0), a3_ss.at[k], a3_rs.at[k], along_y(k))

    def b3_copy(k):
        return remote(part_b(0), part_b(0), b3_ss.at[k], b3_rs.at[k], along_x(k))

    def ca_copy(k):
        return remote(part_a(-k), part_a(-k), ca_ss.at[k], ca_rs.at[k], device(x, y, z, 1 - core))

    def cb_copy(k):
        return remote(part_b(-k), part_b(-k), cb_ss.at[k], cb_rs.at[k], device(x, y, z, 1 - core))

    @pl.loop(1, NX)
    def _(k):
        a2_copy(k).wait()

    @pl.loop(1, NY)
    def _(k):
        a3_copy(k).start()

    @pl.loop(1, NY)
    def _(k):
        b2_copy(k).wait()

    @pl.loop(1, NX)
    def _(k):
        b3_copy(k).start()

    ca_copy(0).start()
    cb_copy(0).start()

    @pl.loop(1, NX)
    def _(k):
        bx_copy(k).wait()

    bias_xin[0] = bias_b[0]
    bias_b[1] = jnp.sum(bias_xin[...], axis=0)

    @pl.loop(1, NZ)
    def _(k):
        bz_copy(k).start()

    @pl.loop(1, NZ)
    def _(k):
        bz_copy(k).wait()

    bias_zin[0] = bias_b[1]
    bias_c[me_group] = jnp.sum(bias_zin[...], axis=0)
    bias_mine = bias_c.at[me_group]

    def bd_copy(k):
        return remote(bias_mine, bias_mine, bd_ss.at[k], bd_rs.at[k], member(k)[2])

    @pl.loop(1, GROUP)
    def _(k):
        bd_copy(k).start()

    for c in ret[2:]:
        c.wait()
    for i, ref in enumerate((gk, gval)):
        back = jnp.concatenate([rcv_l[i, :80], rcv_r[i, :80]], axis=0)
        total = acc_mid[i, RAD * CW : (RAD + CH) * CW] + dot(pack_ref[...], back, TN)
        gap = jnp.zeros((CELLS - RAD * CW, D), F32)
        above = up_in[i].astype(F32).reshape(RAD * CW, D)
        below = down_in[i].astype(F32).reshape(RAD * CW, D)
        total = total + jnp.concatenate([above, gap], axis=0) + jnp.concatenate([gap, below], axis=0)
        ref[...] = total.astype(BF)

    @pl.loop(1, NY)
    def _(k):
        a3_copy(k).wait()
        ca_copy(k).start()
        b3_copy(k).wait()
        cb_copy(k).start()

    @pl.loop(1, GROUP)
    def _(k):
        bd_copy(k).wait()

    ob_ref[...] = jnp.concatenate([bias_c[i, :per, : KS * KS] for i in range(GROUP)], axis=0)

    @pl.loop(0, NY)
    def _(k):
        ca_copy(k).wait()
        cb_copy(k).wait()


def hand_over(*refs):
    sources, targets, sems = refs[:5], refs[5:10], refs[10]
    pairs = [(sources[i], targets[i]) for i in (0, 1, 2, 4)]
    for c in range(CORES):
        for i in range(2):
            for j in range(2):
                first = c * OUTS + i * OUTS // 2 + j * 128
                pairs.append((sources[3].at[c, i, :, :, j], targets[3].at[:, :, :, first : first + 128]))
    copies = [pltpu.make_async_copy(src, dst, sems.at[i]) for i, (src, dst) in enumerate(pairs)]
    for c in copies:
        c.start()
    for c in copies:
        c.wait()


def on_device(queries, keys, values, grad_out, out_weight, rel_bias):
    one_hot, places, pack, strip, spread, join, heads = tables()
    cells_out = jax.ShapeDtypeStruct((CELLS, D), BF)
    dma = pltpu.SemaphoreType.DMA
    vm = pltpu.VMEM
    in_hbm = pl.BlockSpec(memory_space=pltpu.HBM)
    in_vmem = pl.BlockSpec(memory_space=pltpu.VMEM)
    scratch = [
        vm((CH, CW, D), BF),
        vm((CH, CW, D), BF),
        vm((D, D), BF),
        vm((BQ, KEYS, 128), BF),
        vm((2, EXT, CW, D), BF),
        vm((2, 80, D), BF),
        vm((2, 80, D), BF),
        vm((2, 64, D), BF),
        vm((2, 64, D), BF),
        vm((2, STAGE, D), BF),
        vm((2, STAGE, D), BF),
        vm((CELLS, D), BF),
        vm((BLOCKS, KEYS, D), BF),
        vm((BLOCKS, KEYS, D), BF),
        vm((HEADS, BQ, KEYS), F32),
        vm((16, 4 * BQ, KEYS), F32),
        vm((CELLS, D), BF),
        vm((GROUP, CELLS, FEATS), BF),
        vm((GROUP, CH, CW, OUTS), BF),
        vm((HEADS, BQ, KEYS), F32),
        vm((2, EXT * CW, D), F32),
        vm((2, BLOCKS * 2 * SIDEK, D), BF),
        vm((2, STAGE, D), BF),
        vm((2, STAGE, D), BF),
        vm((2, STAGE, D), BF),
        vm((2, STAGE, D), BF),
        vm((2, RAD, CW, D), BF),
        vm((2, RAD, CW, D), BF),
        vm((2, RAD, CW, D), BF),
        vm((2, RAD, CW, D), BF),
        vm((FEATS // PROWS, PROWS, OUTS), BF),
        vm((NX, XPIECES, PROWS, OUTS), BF),
        vm((NZ, PROWS, 256), BF),
        vm((NZ, PROWS, 256), BF),
        vm((GROUP, 8, 128), F32),
        vm((GROUP, 8, 128), F32),
        vm((NX, 8, 128), F32),
        vm((2, 8, 128), F32),
        vm((NZ, 8, 128), F32),
        vm((GROUP, 8, 128), F32),
        dma((9,)),
    ]
    for count in (6, GROUP, (2, GROUP), 6, NX, NZ, NZ, NX, NY, NY, NX, NY, NX, GROUP, NX, NZ, GROUP):
        shape = count if isinstance(count, tuple) else (count,)
        scratch += [dma(shape), dma(shape)]
    results = pl.pallas_call(
        kernel,
        out_shape=(
            vm((CELLS, D), BF),
            vm((CELLS, D), BF),
            vm((CELLS, D), BF),
            vm((CORES, 2, NY, NX * XPIECES, 2, PROWS, 128), BF),
            vm((HEADS, KS * KS), F32),
        ),
        in_specs=[in_hbm] * 5 + [in_vmem, in_hbm] + [in_vmem] * 6,
        out_specs=(in_vmem,) * 5,
        scratch_shapes=scratch,
        compiler_params=pltpu.CompilerParams(
            collective_id=0, has_side_effects=True, vmem_limit_bytes=56 * 2**20
        ),
        cost_estimate=pl.CostEstimate(flops=3 * 10**9, bytes_accessed=8 * 2**20, transcendentals=10**6),
        name="attention_backward",
    )(queries, keys, values, grad_out, out_weight, rel_bias, one_hot, places, pack, strip, spread, join, heads)
    gq, gk, gv, gw, gb = pl.pallas_call(
        hand_over,
        out_shape=(
            cells_out,
            cells_out,
            cells_out,
            jax.ShapeDtypeStruct((NY, FEATS // PROWS, PROWS, D), BF),
            jax.ShapeDtypeStruct((HEADS, KS * KS), F32),
        ),
        in_specs=[in_vmem] * 5,
        out_specs=(in_hbm,) * 5,
        scratch_shapes=[dma((4 + 4 * CORES,))],
        name="hand_over",
    )(*(pltpu.with_memory_space_constraint(r, pltpu.VMEM) for r in results))
    shape = queries.shape
    return gq.reshape(shape), gk.reshape(shape), gv.reshape(shape), gw.reshape(D, D), gb


def solution(mesh):
    cells = P("row", "col", None)
    return jax.shard_map(
        on_device,
        mesh=mesh,
        in_specs=(cells, cells, cells, cells, P(), P()),
        out_specs=(cells, cells, cells, P(), P()),
        check_vma=False,
    )
```

```python
import functools
import math

import jax
import jax.numpy as jnp
import numpy as np
from jax import lax
from jax.experimental import pallas as pl
from jax.experimental.pallas import tpu as pltpu
from jax.sharding import PartitionSpec as P

MESH = pl.DeviceIdType.MESH
BF = jnp.bfloat16
F32 = jnp.float32

RAD = 5
KS = 11
D = 1024
HEADS = 16
CH = 16
CW = 8
CELLS = CH * CW
XLO, NY, NZ, XHI, CORES = 2, 4, 8, 2, 2
NX = XLO * XHI
GROUP = NY * CORES
BLOCKS = 4
BROWS = CH // BLOCKS
BQ = BROWS * CW
MIDK = (BROWS + 2 * RAD) * CW
SIDEK = 72
KEYS = MIDK + 2 * SIDEK
STAGE = 144
EXT = CH + 2 * RAD
FEATS = D // NY
OUTS = D // CORES
PROWS = 16
XPIECES = FEATS // PROWS // NX
NEG = -1e30
NEIGHBOURS = ((0, -1), (0, 1), (-1, 0), (1, 0))


def key_places():
    rows = np.full(KEYS, 1000, np.int64)
    cols = np.full(KEYS, 1000, np.int64)
    mid = np.arange(MIDK)
    rows[:MIDK], cols[:MIDK] = mid // CW, mid % CW
    side = np.arange(70)
    for first, base in ((MIDK, -RAD), (MIDK + SIDEK, CW)):
        rows[first + 1 : first + 71] = side // RAD
        cols[first + 1 : first + 71] = base + side % RAD
    return rows, cols


def tables():
    rows, cols = key_places()
    query = np.arange(BQ)
    dr = rows[None, :] - RAD - (query // CW)[:, None]
    dc = cols[None, :] - (query % CW)[:, None]
    inside = (np.abs(dr) <= RAD) & (np.abs(dc) <= RAD)
    offsets = np.where(inside, (dr + RAD) * KS + dc + RAD, 127)
    one_hot = offsets[:, :, None] == np.arange(128)[None, None, :]
    places = np.zeros((8, KEYS), np.int32)
    places[0], places[1] = rows, cols
    pack = np.zeros((2 * 80, CELLS), bool)
    edge = np.arange(80)
    pack[edge, edge // RAD * CW + edge % RAD] = True
    pack[80 + edge, edge // RAD * CW + CW - RAD + edge % RAD] = True
    spread = np.zeros((BLOCKS * SIDEK, STAGE), bool)
    place = np.arange(70)
    for b in range(BLOCKS):
        ext = 20 * b + place
        at = np.where(ext < 25, 80 + ext, np.where(ext < 105, ext - 25, ext))
        spread[b * SIDEK + 1 + place, at] = True
    strip = np.zeros((2 * 64, 2 * RAD * CW), bool)
    corner = np.arange(50)
    strip[corner, corner // RAD * CW + corner % RAD] = True
    strip[64 + corner, corner // RAD * CW + CW - RAD + corner % RAD] = True
    join = np.zeros((2 * STAGE, BLOCKS * 2 * SIDEK), bool)
    for b in range(BLOCKS):
        at = spread[b * SIDEK : (b + 1) * SIDEK].T
        join[:STAGE, 2 * SIDEK * b : 2 * SIDEK * b + SIDEK] = at
        join[STAGE:, 2 * SIDEK * b + SIDEK : 2 * SIDEK * (b + 1)] = at
    heads = np.repeat(np.arange(4), BQ)[:, None] == (np.arange(256) // 64)[None, :]
    as_low = lambda t: np.asarray(t, np.float32).astype(jnp.bfloat16)
    return (as_low(one_hot), places, as_low(pack), as_low(strip), as_low(spread), as_low(join), as_low(heads))


def dot(a, b, dims):
    return lax.dot_general(a, b, ((dims[0], dims[1]), ((), ())), preferred_element_type=F32)


NN = ((1,), (0,))
NT = ((1,), (1,))
TN = ((0,), (0,))


def kernel(
    q_hbm, k_hbm, v_hbm, g_hbm, w_hbm, bias_ref, oh_hbm, places_ref, pack_ref, strip_ref, spread_ref, join_ref, heads_ref,
    gq, gk, gval, out, ob_ref,
    qv, gv, wv, ohv, mid, panel_l, panel_r, strip_l, strip_r, stage_l, stage_r, ga, kb, vb, table, probs, att, at, go,
    sg_sum, acc_mid, side, ret_l, ret_r, rcv_l, rcv_r, up_out, down_out, up_in, down_in,
    wt, rx, wz, rz, bias_a, bias_ain, bias_xin, bias_b, bias_zin, bias_c,
    loc_sem, halo_ss, halo_rs, go_ss, go_rs, at_ss, at_rs, ret_ss, ret_rs, rx_ss, rx_rs, rz_ss, rz_rs, zg_ss, zg_rs,
    a2_ss, a2_rs, b2_ss, b2_rs, a3_ss, a3_rs, b3_ss, b3_rs, ca_ss, ca_rs, cb_ss, cb_rs,
    ba_ss, ba_rs, bx_ss, bx_rs, bz_ss, bz_rs, bd_ss, bd_rs,
):
    row, col = lax.axis_index("row"), lax.axis_index("col")
    nrow, ncol = XLO * NY, NZ * XHI * CORES
    x = (col // CORES) % XHI * XLO + row // NY
    y, z, core = row % NY, col // (XHI * CORES), col % CORES
    scale = 1.0 / math.sqrt(D // HEADS)

    def device(x_at, y_at, z_at, core_at):
        return (x_at % XLO * NY + y_at, (z_at * XHI + x_at // XLO) * CORES + core_at)

    def neighbour(dr, dc):
        return ((row + dr + nrow) % nrow, (col + dc + ncol) % ncol)

    def member(k):
        yy = (y + k // CORES) % NY
        cc = (core + k % CORES) % CORES
        return yy, cc, device(x, yy, z, cc)

    def along_x(k):
        return device((x + k) % NX, y, z, core)

    def along_y(k):
        return device(x, (y + k) % NY, z, core)

    def along_z(k):
        return device(x, y, (z + k) % NZ, core)

    me_group = y * CORES + core

    def local(src, dst, at_sem):
        return pltpu.make_async_copy(src, dst, loc_sem.at[at_sem])

    def remote(src, dst, ss, rsem, to):
        return pltpu.make_async_remote_copy(
            src_ref=src, dst_ref=dst, send_sem=ss, recv_sem=rsem, device_id=to, device_id_type=MESH
        )

    loads = [
        local(k_hbm, mid.at[0, RAD : RAD + CH], 0),
        local(v_hbm, mid.at[1, RAD : RAD + CH], 1),
        local(g_hbm, gv, 2),
        local(w_hbm, wv, 3),
        local(q_hbm, qv, 4),
        local(oh_hbm, ohv, 5),
    ]
    for c in loads:
        c.start()
    barrier = pltpu.get_barrier_semaphore()
    for dr, dc in NEIGHBOURS:
        pl.semaphore_signal(barrier, inc=1, device_id=neighbour(dr, dc), device_id_type=MESH)

    @pl.loop(1, GROUP)
    def _(k):
        pl.semaphore_signal(barrier, inc=1, device_id=member(k)[2], device_id_type=MESH)

    @pl.loop(1, NX)
    def _(k):
        pl.semaphore_signal(barrier, inc=1, device_id=along_x(k), device_id_type=MESH)

    @pl.loop(1, NZ)
    def _(k):
        pl.semaphore_signal(barrier, inc=1, device_id=along_z(k), device_id_type=MESH)

    loads[0].wait()
    loads[1].wait()
    for i in range(2):
        own = mid[i, RAD : RAD + CH].reshape(CELLS, D)
        packed = dot(pack_ref[...], own, NN).astype(BF)
        panel_l[i] = packed[:80]
        panel_r[i] = packed[80:]
    pl.semaphore_wait(barrier, len(NEIGHBOURS) + GROUP - 1 + NX - 1 + NZ - 1)

    halo_parts = (
        (mid.at[:, RAD : 2 * RAD], mid.at[:, RAD + CH :], 2),
        (mid.at[:, CH : CH + RAD], mid.at[:, :RAD], 3),
        (panel_l, stage_r.at[:, :80], 0),
        (panel_r, stage_l.at[:, :80], 1),
        (strip_l, stage_r.at[:, 80:], 0),
        (strip_r, stage_l.at[:, 80:], 1),
    )
    halo = [
        remote(src, dst, halo_ss.at[i], halo_rs.at[i], neighbour(*NEIGHBOURS[n]))
        for i, (src, dst, n) in enumerate(halo_parts)
    ]
    for c in halo[:4]:
        c.start()

    loads[2].wait()

    def go_copy(k):
        yy, cc, to = member(k)
        lanes = pl.ds(pl.multiple_of(cc * OUTS, OUTS), OUTS)
        return remote(gv.at[:, :, lanes], go.at[me_group], go_ss.at[k], go_rs.at[k], to)

    @pl.loop(1, GROUP)
    def _(k):
        go_copy(k).start()

    own_lanes = pl.ds(pl.multiple_of(core * OUTS, OUTS), OUTS)
    go_own = local(gv.at[:, :, own_lanes], go.at[me_group], 6)
    go_own.start()

    loads[3].wait()
    ga[...] = dot(gv[...].reshape(CELLS, D), wv[...], NT).astype(BF)

    halo[0].wait()
    halo[1].wait()
    for i in range(2):
        rims = jnp.concatenate([mid[i, :RAD], mid[i, RAD + CH :]], axis=0).reshape(2 * RAD * CW, D)
        packed = dot(strip_ref[...], rims, NN).astype(BF)
        strip_l[i] = packed[:64]
        strip_r[i] = packed[64:]
    halo[4].start()
    halo[5].start()

    loads[5].wait()
    padded = jnp.concatenate([bias_ref[...], jnp.full((HEADS, 128 - KS * KS), NEG, F32)], axis=1)
    high = padded.astype(BF)
    rest = padded - high.astype(F32)
    middle = rest.astype(BF)
    low = (rest - middle.astype(F32)).astype(BF)
    three = jnp.concatenate([high, middle, low], axis=0)
    for i in range(BQ):
        terms = dot(three, ohv[i], NT)
        table[:, i, :] = terms[:HEADS] + terms[HEADS : 2 * HEADS] + terms[2 * HEADS :]
    for ref in (acc_mid, sg_sum):
        ref[...] = jnp.zeros_like(ref)

    for i, slab in enumerate((kb, vb)):
        for b in range(BLOCKS):
            slab[b, :MIDK] = mid[i, b * BROWS : b * BROWS + BROWS + 2 * RAD].reshape(MIDK, D)
    loads[4].wait()
    for c in halo[2:]:
        c.wait()
    for i, slab in enumerate((kb, vb)):
        left = dot(spread_ref[...], stage_l[i], NN)
        right = dot(spread_ref[...], stage_r[i], NN)
        for b in range(BLOCKS):
            rows = slice(b * SIDEK, (b + 1) * SIDEK)
            slab[b, MIDK:] = jnp.concatenate([left[rows], right[rows]], axis=0).astype(BF)

    mask_low = heads_ref[...]
    mask_wide = mask_low.astype(F32)

    def spread_heads(tile):
        return jnp.concatenate([tile] * 4, axis=0) * mask_low

    def fold_heads(full):
        return jnp.sum((full * mask_wide).reshape(4, BQ, 256), axis=0)

    key_row, key_col = places_ref[0:1, :], places_ref[1:2, :]
    grid_col = col * CW + key_col
    col_ok = (grid_col >= 0) & (grid_col < ncol * CW)
    q2 = qv[...].reshape(CELLS, D)
    groups = [slice(h * 256, (h + 1) * 256) for h in range(4)]

    def forward(b):
        cells = slice(b * BQ, (b + 1) * BQ)
        grid_row = row * CH + b * BROWS - RAD + key_row
        present = col_ok & (grid_row >= 0) & (grid_row < nrow * CH)
        absent = jnp.where(present, 0.0, NEG)
        scores = [dot(spread_heads(q2[cells, n]), kb[b, :, n], NT) for n in groups]
        scores = [
            s * scale + (table[4 * h : 4 * h + 4].reshape(4 * BQ, KEYS) + absent) for h, s in enumerate(scores)
        ]
        weights = [jnp.exp(s - jnp.max(s, axis=1, keepdims=True)) for s in scores]
        p = [e * (1.0 / jnp.sum(e, axis=1, keepdims=True)) for e in weights]
        for h in range(4):
            probs[b * 4 + h] = p[h]
        full = [dot(t.astype(BF), vb[b, :, n], NN) for t, n in zip(p, groups)]
        for t, n in zip(full, groups):
            att[cells, n] = fold_heads(t).astype(BF)

    half_cells = CELLS // 2

    def at_copy(part, k):
        yy, cc, to = member(k)
        src = att.at[pl.ds(part * half_cells, half_cells), pl.ds(pl.multiple_of(yy * FEATS, FEATS), FEATS)]
        dst = at.at[me_group, pl.ds(part * half_cells, half_cells)]
        return remote(src, dst, at_ss.at[part, k], at_rs.at[part, k], to)

    for part in range(2):
        forward(2 * part)
        forward(2 * part + 1)

        @pl.loop(1, GROUP)
        def _(k):
            at_copy(part, k).start()

    at_own = local(att.at[:, pl.ds(pl.multiple_of(y * FEATS, FEATS), FEATS)], at.at[me_group], 7)
    at_own.start()

    def backward(b):
        cells = slice(b * BQ, (b + 1) * BQ)
        qm = [spread_heads(q2[cells, n]) for n in groups]
        gm = [spread_heads(ga[cells, n]) for n in groups]
        p = [probs[b * 4 + h] for h in range(4)]
        dp = [dot(g, vb[b, :, n], NT) for g, n in zip(gm, groups)]
        sg = [t * (d - jnp.sum(t * d, axis=1, keepdims=True)) for t, d in zip(p, dp)]
        for h in range(4):
            sg_sum[4 * h : 4 * h + 4] += sg[h].reshape(4, BQ, KEYS)
        sl = [t.astype(BF) for t in sg]
        for h, n in enumerate(groups):
            gq[cells, n] = (fold_heads(dot(sl[h], kb[b, :, n], NN)) * scale).astype(BF)
            parts = (dot(sl[h], qm[h], TN) * scale, dot(p[h].astype(BF), gm[h], TN))
            for i, part in enumerate(parts):
                acc_mid[i, b * BQ : b * BQ + MIDK, n] += part[:MIDK]
                side[i, b * 2 * SIDEK : (b + 1) * 2 * SIDEK, n] = part[MIDK:].astype(BF)

    backward(0)
    backward(1)
    go_own.wait()
    at_own.wait()

    @pl.loop(1, GROUP)
    def _(k):
        go_copy(k).wait()
        at_copy(0, k).wait()
        at_copy(1, k).wait()

    wt[...] = dot(at[...].reshape(GROUP * CELLS, FEATS), go[...].reshape(GROUP * CELLS, OUTS), TN).reshape(FEATS // PROWS, PROWS, OUTS).astype(BF)

    def rx_copy(k):
        part = wt.at[pl.ds((x + k) % NX * XPIECES, XPIECES)]
        return remote(part, rx.at[k], rx_ss.at[k], rx_rs.at[k], along_x(k))

    @pl.loop(1, NX)
    def _(k):
        rx_copy(k).start()

    rx_own = local(wt.at[pl.ds(x * XPIECES, XPIECES)], rx.at[0], 8)
    rx_own.start()
    backward(2)
    backward(3)

    for i in range(2):
        joined = dot(join_ref[...], side[i], NN).astype(BF)
        ret_l[i] = joined[:STAGE]
        ret_r[i] = joined[STAGE:]
    ret_parts = (
        (ret_l.at[:, 80:], rcv_r.at[:, 80:], 0),
        (ret_r.at[:, 80:], rcv_l.at[:, 80:], 1),
        (ret_l.at[:, :80], rcv_r.at[:, :80], 0),
        (ret_r.at[:, :80], rcv_l.at[:, :80], 1),
        (up_out, down_in, 2),
        (down_out, up_in, 3),
    )
    ret = [
        remote(src, dst, ret_ss.at[i], ret_rs.at[i], neighbour(*NEIGHBOURS[n]))
        for i, (src, dst, n) in enumerate(ret_parts)
    ]

    rx_own.wait()

    @pl.loop(1, NX)
    def _(k):
        rx_copy(k).wait()

    total = jnp.sum(rx[...].astype(F32), axis=0).astype(BF)
    half = OUTS // 2
    for i in range(XPIECES):
        for j in range(2):
            first, second = total[i, :, j * 128 : j * 128 + 128], total[i, :, half + j * 128 : half + j * 128 + 128]
            wz[2 * i + j] = jnp.concatenate([first, second], axis=1)

    def rz_copy(k):
        return remote(wz.at[(z + k) % NZ], rz.at[k], rz_ss.at[k], rz_rs.at[k], along_z(k))

    @pl.loop(1, NZ)
    def _(k):
        rz_copy(k).start()

    for c in ret[:4]:
        c.start()

    rz[0] = wz[z]

    @pl.loop(1, NZ)
    def _(k):
        rz_copy(k).wait()

    final = jnp.sum(rz[...].astype(F32), axis=0).astype(BF)
    spot = x * XPIECES + z // 2
    out[core, 0, y, spot, z % 2] = final[:, :128]
    out[core, 1, y, spot, z % 2] = final[:, 128:]
    mine = out.at[core, :, y, spot, z % 2]

    def zg_copy(k):
        return remote(mine, mine, zg_ss.at[k], zg_rs.at[k], along_z(k))

    @pl.loop(1, NZ)
    def _(k):
        zg_copy(k).start()

    bias_sum = jnp.zeros((2 * HEADS, 128), F32)
    for i in range(BQ):
        sums = sg_sum[:, i, :]
        high = sums.astype(BF)
        low = (sums - high.astype(F32)).astype(BF)
        bias_sum = bias_sum + dot(jnp.concatenate([high, low], axis=0), ohv[i], NN)
    bias_sum = bias_sum[:HEADS] + bias_sum[HEADS:]
    per = HEADS // GROUP
    bias_a[...] = jnp.zeros_like(bias_a)
    for i in range(GROUP):
        bias_a[i, :per] = bias_sum[i * per : (i + 1) * per]

    def ba_copy(k):
        yy, cc, to = member(k)
        return remote(bias_a.at[yy * CORES + cc], bias_ain.at[k], ba_ss.at[k], ba_rs.at[k], to)

    @pl.loop(1, GROUP)
    def _(k):
        ba_copy(k).start()

    @pl.loop(1, NZ)
    def _(k):
        zg_copy(k).wait()

    slab_a = out.at[core, 0, y, pl.ds(x * XPIECES, XPIECES)]
    slab_b = out.at[core, 1, y, pl.ds(x * XPIECES, XPIECES)]

    def a2_copy(k):
        return remote(slab_a, slab_a, a2_ss.at[k], a2_rs.at[k], along_x(k))

    def b2_copy(k):
        return remote(slab_b, slab_b, b2_ss.at[k], b2_rs.at[k], along_y(k))

    @pl.loop(1, NY)
    def _(k):
        b2_copy(k).start()

    @pl.loop(1, NX)
    def _(k):
        a2_copy(k).start()

    ret[0].wait()
    ret[1].wait()
    for i in range(2):
        back = jnp.concatenate([rcv_l[i, 80:], rcv_r[i, 80:]], axis=0)
        corners = dot(strip_ref[...], back, TN)
        rim = RAD * CW
        up_out[i] = (acc_mid[i, :rim] + corners[:rim]).reshape(RAD, CW, D).astype(BF)
        down_out[i] = (acc_mid[i, rim + CELLS :] + corners[rim:]).reshape(RAD, CW, D).astype(BF)
    ret[4].start()
    ret[5].start()

    @pl.loop(1, GROUP)
    def _(k):
        ba_copy(k).wait()

    bias_ain[0] = bias_a[me_group]
    bias_b[0] = jnp.sum(bias_ain[...], axis=0)

    def bx_copy(k):
        return remote(bias_b.at[0], bias_xin.at[k], bx_ss.at[k], bx_rs.at[k], along_x(k))

    def bz_copy(k):
        return remote(bias_b.at[1], bias_zin.at[k], bz_ss.at[k], bz_rs.at[k], along_z(k))

    @pl.loop(1, NX)
    def _(k):
        bx_copy(k).start()

    def part_a(k):
        return out.at[core, 0, (y + k + NY) % NY]

    def part_b(k):
        return out.at[core, 1, :, pl.ds((x + k + NX) % NX * XPIECES, XPIECES)]

    def a3_copy(k):
        return remote(part_a(0), part_a(0), a3_ss.at[k], a3_rs.at[k], along_y(k))

    def b3_copy(k):
        return remote(part_b(0), part_b(0), b3_ss.at[k], b3_rs.at[k], along_x(k))

    def ca_copy(k):
        return remote(part_a(-k), part_a(-k), ca_ss.at[k], ca_rs.at[k], device(x, y, z, 1 - core))

    def cb_copy(k):
        return remote(part_b(-k), part_b(-k), cb_ss.at[k], cb_rs.at[k], device(x, y, z, 1 - core))

    @pl.loop(1, NX)
    def _(k):
        a2_copy(k).wait()

    @pl.loop(1, NY)
    def _(k):
        a3_copy(1 + k % (NY - 1)).start()

    @pl.loop(1, NY)
    def _(k):
        b2_copy(k).wait()

    @pl.loop(1, NX)
    def _(k):
        b3_copy(1 + k % (NX - 1)).start()

    ca_copy(0).start()
    cb_copy(0).start()

    @pl.loop(1, NX)
    def _(k):
        bx_copy(k).wait()

    bias_xin[0] = bias_b[0]
    bias_b[1] = jnp.sum(bias_xin[...], axis=0)

    @pl.loop(1, NZ)
    def _(k):
        bz_copy(k).start()

    @pl.loop(1, NZ)
    def _(k):
        bz_copy(k).wait()

    bias_zin[0] = bias_b[1]
    bias_c[me_group] = jnp.sum(bias_zin[...], axis=0)
    bias_mine = bias_c.at[me_group]

    def bd_copy(k):
        return remote(bias_mine, bias_mine, bd_ss.at[k], bd_rs.at[k], member(k)[2])

    @pl.loop(1, GROUP)
    def _(k):
        bd_copy(k).start()

    for c in ret[2:]:
        c.wait()
    for i, ref in enumerate((gk, gval)):
        back = jnp.concatenate([rcv_l[i, :80], rcv_r[i, :80]], axis=0)
        total = acc_mid[i, RAD * CW : (RAD + CH) * CW] + dot(pack_ref[...], back, TN)
        gap = jnp.zeros((CELLS - RAD * CW, D), F32)
        above = up_in[i].astype(F32).reshape(RAD * CW, D)
        below = down_in[i].astype(F32).reshape(RAD * CW, D)
        total = total + jnp.concatenate([above, gap], axis=0) + jnp.concatenate([gap, below], axis=0)
        ref[...] = total.astype(BF)

    @pl.loop(1, NY)
    def _(k):
        a3_copy(k).wait()
        ca_copy(k).start()
        b3_copy(k).wait()
        cb_copy(k).start()

    @pl.loop(1, GROUP)
    def _(k):
        bd_copy(k).wait()

    ob_ref[...] = jnp.concatenate([bias_c[i, :per, : KS * KS] for i in range(GROUP)], axis=0)

    @pl.loop(0, NY)
    def _(k):
        ca_copy(k).wait()
        cb_copy(k).wait()


def hand_over(*refs):
    sources, targets, sems = refs[:5], refs[5:10], refs[10]
    pairs = [(sources[i], targets[i]) for i in (0, 1, 2, 4)]
    for c in range(CORES):
        for i in range(2):
            for j in range(2):
                first = c * OUTS + i * OUTS // 2 + j * 128
                pairs.append((sources[3].at[c, i, :, :, j], targets[3].at[:, :, :, first : first + 128]))
    copies = [pltpu.make_async_copy(src, dst, sems.at[i]) for i, (src, dst) in enumerate(pairs)]
    for c in copies:
        c.start()
    for c in copies:
        c.wait()


def on_device(queries, keys, values, grad_out, out_weight, rel_bias):
    one_hot, places, pack, strip, spread, join, heads = tables()
    cells_out = jax.ShapeDtypeStruct((CELLS, D), BF)
    dma = pltpu.SemaphoreType.DMA
    vm = pltpu.VMEM
    in_hbm = pl.BlockSpec(memory_space=pltpu.HBM)
    in_vmem = pl.BlockSpec(memory_space=pltpu.VMEM)
    scratch = [
        vm((CH, CW, D), BF),
        vm((CH, CW, D), BF),
        vm((D, D), BF),
        vm((BQ, KEYS, 128), BF),
        vm((2, EXT, CW, D), BF),
        vm((2, 80, D), BF),
        vm((2, 80, D), BF),
        vm((2, 64, D), BF),
        vm((2, 64, D), BF),
        vm((2, STAGE, D), BF),
        vm((2, STAGE, D), BF),
        vm((CELLS, D), BF),
        vm((BLOCKS, KEYS, D), BF),
        vm((BLOCKS, KEYS, D), BF),
        vm((HEADS, BQ, KEYS), F32),
        vm((16, 4 * BQ, KEYS), F32),
        vm((CELLS, D), BF),
        vm((GROUP, CELLS, FEATS), BF),
        vm((GROUP, CH, CW, OUTS), BF),
        vm((HEADS, BQ, KEYS), F32),
        vm((2, EXT * CW, D), F32),
        vm((2, BLOCKS * 2 * SIDEK, D), BF),
        vm((2, STAGE, D), BF),
        vm((2, STAGE, D), BF),
        vm((2, STAGE, D), BF),
        vm((2, STAGE, D), BF),
        vm((2, RAD, CW, D), BF),
        vm((2, RAD, CW, D), BF),
        vm((2, RAD, CW, D), BF),
        vm((2, RAD, CW, D), BF),
        vm((FEATS // PROWS, PROWS, OUTS), BF),
        vm((NX, XPIECES, PROWS, OUTS), BF),
        vm((NZ, PROWS, 256), BF),
        vm((NZ, PROWS, 256), BF),
        vm((GROUP, 8, 128), F32),
        vm((GROUP, 8, 128), F32),
        vm((NX, 8, 128), F32),
        vm((2, 8, 128), F32),
        vm((NZ, 8, 128), F32),
        vm((GROUP, 8, 128), F32),
        dma((9,)),
    ]
    for count in (6, GROUP, (2, GROUP), 6, NX, NZ, NZ, NX, NY, NY, NX, NY, NX, GROUP, NX, NZ, GROUP):
        shape = count if isinstance(count, tuple) else (count,)
        scratch += [dma(shape), dma(shape)]
    results = pl.pallas_call(
        kernel,
        out_shape=(
            vm((CELLS, D), BF),
            vm((CELLS, D), BF),
            vm((CELLS, D), BF),
            vm((CORES, 2, NY, NX * XPIECES, 2, PROWS, 128), BF),
            vm((HEADS, KS * KS), F32),
        ),
        in_specs=[in_hbm] * 5 + [in_vmem, in_hbm] + [in_vmem] * 6,
        out_specs=(in_vmem,) * 5,
        scratch_shapes=scratch,
        compiler_params=pltpu.CompilerParams(
            collective_id=0, has_side_effects=True, vmem_limit_bytes=56 * 2**20
        ),
        cost_estimate=pl.CostEstimate(flops=3 * 10**9, bytes_accessed=8 * 2**20, transcendentals=10**6),
        name="attention_backward",
    )(queries, keys, values, grad_out, out_weight, rel_bias, one_hot, places, pack, strip, spread, join, heads)
    gq, gk, gv, gw, gb = pl.pallas_call(
        hand_over,
        out_shape=(
            cells_out,
            cells_out,
            cells_out,
            jax.ShapeDtypeStruct((NY, FEATS // PROWS, PROWS, D), BF),
            jax.ShapeDtypeStruct((HEADS, KS * KS), F32),
        ),
        in_specs=[in_vmem] * 5,
        out_specs=(in_hbm,) * 5,
        scratch_shapes=[dma((4 + 4 * CORES,))],
        name="hand_over",
    )(*(pltpu.with_memory_space_constraint(r, pltpu.VMEM) for r in results))
    shape = queries.shape
    return gq.reshape(shape), gk.reshape(shape), gv.reshape(shape), gw.reshape(D, D), gb


def solution(mesh):
    cells = P("row", "col", None)
    return jax.shard_map(
        on_device,
        mesh=mesh,
        in_specs=(cells, cells, cells, cells, P(), P()),
        out_specs=(cells, cells, cells, P(), P()),
        check_vma=False,
    )
```
